256 devices in a mesh: dp: 16 (over y, z_lo), tensor: 16 (over z_hi, x, core).
Axes of the slice: x: 4, y: 4, z: 8 (z_hi: 2, z_lo: 4; z = z_hi * 4 + z_lo), core: 2. Of those that a mesh axis runs over, the one named last changes fastest.
Arguments:
- tokens: bfloat16 [4096, 4096], P('dp'), may hold values from -6 to 6
- cotangent: bfloat16 [4096, 4096], P('dp'), may hold values from -0.1875 to 0.1875
- up_weight_kept: bfloat16 [4096, 14336], P('dp', 'tensor'), may hold values from -0.09375 to 0.09375
- down_weight_kept: bfloat16 [4096, 14336], P('dp', 'tensor'), may hold values from -0.09375 to 0.09375
- first_moment_blocks: float32 [2, 4096, 14336], P(None, 'dp', 'tensor'), may hold values from -6 to 6
- second_moment_blocks: float32 [2, 4096, 14336], P(None, 'dp', 'tensor'), may hold values from 0.5 to 5
- block_destination: int32 [16, 16], replicated, may hold values from 0 to 15, as said below
- surviving_device_rank: int32 [16], replicated, may hold values from 0 to 15, each once
Outputs:
- new_up: bfloat16 [4096, 14336], P('dp', 'tensor')
- new_down: bfloat16 [4096, 14336], P('dp', 'tensor')
- new_first: float32 [2, 4096, 14336], P(None, 'dp', 'tensor')
- new_second: float32 [2, 4096, 14336], P(None, 'dp', 'tensor')
The draws below stay inside these ranges and needn't reach their ends.
Inputs may be any that keep to these rules, and one draw needn't show every extreme that they name: Each row of block_destination names every new tensor index exactly once.
All inputs are finite; a program needn't handle non-finite values.
Results may differ from the reference program's by a relative error of at most 0.0035.
Values may be sent and summed in bfloat16 or wider, within the bound.
A program may use at most 128 MiB of HBM per device.

```python
import math
import jax
import jax.numpy as jnp
from jax import lax

D = 4096
FF = 14336
TOK_DEV = 256
TOKENS = 4096
PIECE = 16
N_DP = 16
N_TENSOR = 16


def draw_block_destination(key, part):
    key = jax.random.fold_in(key, 11)
    keys = jax.random.split(key, N_TENSOR)
    return jax.vmap(lambda sub: jax.random.permutation(sub, N_TENSOR))(keys).astype(jnp.int32)


def shard_levels(stream_key, shape, cuts, smallest, high):
    gain, own = 1.0, jax.random.fold_in(stream_key, 6)
    for position, parts in cuts:
        draws = jnp.exp(jax.random.uniform(jax.random.fold_in(own, position), (parts,), jnp.float32, smallest / len(cuts), high / len(cuts)))
        gain = gain * jnp.repeat(draws, shape[position] // parts).reshape([-1 if axis == position else 1 for axis in range(len(shape))])
    return gain


def gaussian(own_key, extent, scale, reach, pieces=(), kind=jnp.bfloat16):
    loudness = shard_levels(own_key, extent, pieces, -0.22, 0.18) if pieces else 1.0
    drawn = jax.random.normal(own_key, extent, jnp.float32) * scale * loudness
    return jnp.minimum(jnp.maximum(drawn, -reach), reach).astype(kind)


def setup_inputs(seed: int = 0) -> dict:
    arg_keys = jax.random.split(jax.random.key(seed), 9)
    tokens = gaussian(arg_keys[0], (TOKENS, D), 1.0, 6.0, ((0, 16),))
    cotangent = gaussian(arg_keys[1], (TOKENS, D), (2 * TOKENS ** -0.5), 0.1875, ((0, 16),))
    up_weight_kept = gaussian(arg_keys[2], (D, FF), D ** -0.5, 0.09375, ((0, 16), (1, 16)))
    down_weight_kept = gaussian(arg_keys[3], (D, FF), D ** -0.5, 0.09375, ((0, 16), (1, 16)))
    first_moment_blocks = gaussian(arg_keys[4], (2, D, FF), 1.0, 6.0, ((1, 16), (2, 16)), jnp.float32)
    second_moment_blocks = jnp.clip(jnp.exp(math.log(5.0) - 2.3025851 * jax.random.uniform(arg_keys[5], (2, D, FF), jnp.float32) ** shard_levels(arg_keys[5], (2, D, FF), ((1, 16), (2, 16)), -0.2, 0.2)), 0.5, 5.0)
    block_destination = draw_block_destination(jax.random.fold_in(arg_keys[8], 71), 0)
    surviving_device_rank = jax.random.permutation(arg_keys[7], N_TENSOR).astype(jnp.int32)
    return dict(tokens=tokens, cotangent=cotangent, up_weight_kept=up_weight_kept, down_weight_kept=down_weight_kept, first_moment_blocks=first_moment_blocks, second_moment_blocks=second_moment_blocks, block_destination=block_destination, surviving_device_rank=surviving_device_rank)


beta_first = 0.9
beta_second = 0.95
adam_eps = 1e-08
rate = 0.005
step_count = 20

def rounded(value):
    return lax.optimization_barrier(value.astype(jnp.bfloat16)).astype(jnp.float32)

def regroup_layout(kept_blocks, block_destination, surviving_device_rank):
    tensor_groups = N_TENSOR
    width = FF // tensor_groups
    block_positions = jnp.arange(tensor_groups, dtype=jnp.int32)
    inverse_owner = lax.optimization_barrier(jnp.sum(block_positions[None, None, :] * (block_destination[:, None, :] == block_positions[None, :, None]).astype(jnp.int32), axis=2)).astype(jnp.int32)
    placed_blocks = (surviving_device_rank[:, None] + block_positions[None, :]) % tensor_groups
    source = lax.optimization_barrier(jnp.sum(block_positions[:, None, None] * (placed_blocks[:, :, None] == block_positions[None, None, :]).astype(jnp.int32), axis=0)).astype(jnp.int32)
    row_pick = inverse_owner[source, block_positions[:, None]]
    blocks = kept_blocks.reshape(N_DP, tensor_groups, PIECE, tensor_groups, width).transpose(1, 3, 0, 2, 4)
    picked = blocks[row_pick, source]
    return picked.transpose(2, 1, 3, 0, 4).reshape(D, FF)

def block_sum(left, right):
    per = D // N_DP

    def step(index, total):
        start = (jnp.asarray(index, jnp.int32) * per).astype(jnp.int32)
        part = jnp.dot(lax.dynamic_slice_in_dim(left, start, per, 1), lax.dynamic_slice_in_dim(right, start, per, 0), preferred_element_type=jnp.float32)
        return total + rounded(part)
    return lax.fori_loop(0, N_DP, step, jnp.zeros((left.shape[0], right.shape[1]), jnp.float32))

def replica_sum(left, right):

    def step(index, total):
        start = (jnp.asarray(index, jnp.int32) * TOK_DEV).astype(jnp.int32)
        rows_left = lax.dynamic_slice_in_dim(left, start, TOK_DEV, 0)
        rows_right = lax.dynamic_slice_in_dim(right, start, TOK_DEV, 0)
        part = jnp.dot(rows_left.T, rows_right, preferred_element_type=jnp.float32)
        return total + rounded(part)
    return lax.fori_loop(0, N_DP, step, jnp.zeros((left.shape[1], right.shape[1]), jnp.float32))

def adam(weight, first, second, grad):
    first_new = beta_first * first + (1.0 - beta_first) * grad
    second_new = beta_second * second + (1.0 - beta_second) * grad * grad
    first_hat = first_new / (1.0 - beta_first ** step_count)
    second_hat = second_new / (1.0 - beta_second ** step_count)
    updated = weight.astype(jnp.float32) - rate * first_hat / (jnp.sqrt(second_hat) + adam_eps)
    return (updated.astype(jnp.bfloat16), first_new, second_new)

def reference(tokens, cotangent, up_weight_kept, down_weight_kept, first_moment_blocks, second_moment_blocks, block_destination, surviving_device_rank):
    up_weight = regroup_layout(up_weight_kept, block_destination, surviving_device_rank)
    down_weight = regroup_layout(down_weight_kept, block_destination, surviving_device_rank)
    up_first_moment = regroup_layout(first_moment_blocks[0], block_destination, surviving_device_rank)
    down_first_moment = regroup_layout(first_moment_blocks[1], block_destination, surviving_device_rank)
    up_second_moment = regroup_layout(second_moment_blocks[0], block_destination, surviving_device_rank)
    down_second_moment = regroup_layout(second_moment_blocks[1], block_destination, surviving_device_rank)
    pre = block_sum(tokens, up_weight)
    back = block_sum(cotangent, down_weight)
    sigma = jax.nn.sigmoid(pre)
    hidden = (pre * sigma).astype(jnp.bfloat16)
    slope = (back * sigma * (1.0 + pre * (1.0 - sigma))).astype(jnp.bfloat16)
    grad_up = replica_sum(tokens, slope)
    grad_down = replica_sum(cotangent, hidden)
    new_up, f_up, s_up = adam(up_weight, up_first_moment, up_second_moment, grad_up)
    new_down, f_down, s_down = adam(down_weight, down_first_moment, down_second_moment, grad_down)
    return (new_up, new_down, jnp.stack([f_up, f_down]), jnp.stack([s_up, s_down]))
```

```python
import jax
import jax.numpy as jnp
from jax import lax
from jax.experimental import pallas as pl
from jax.experimental.pallas import tpu as pltpu
from jax.sharding import PartitionSpec as P

beta_first = 0.9
beta_second = 0.95
adam_eps = 1e-08
rate = 0.005
step_count = 20

MESH = pl.DeviceIdType.MESH
BF = jnp.bfloat16
F32 = jnp.float32

N = 16
PIECE = 16
ROWS = 256
WIDTH = 896
QUART = 224
D = 4096
TOK = 1024
CHUNK = 1024
PART = 32


def wait_bytes(ref, sem):
    pltpu.make_async_copy(ref, ref, sem).wait()


def exchange(
    bd,
    rank,
    tok,
    cot,
    upk,
    dnk,
    fst,
    snd,
    momr,
    gout,
    X,
    stg,
    wst,
    wq,
    wr,
    mom,
    wall,
    acc,
    act,
    gp,
    relay,
    got,
    gsum,
    order,
    pick,
    loc,
    t1s,
    t1r,
    t2s,
    t2r,
    t3s,
    t3r,
    wqs,
    wqr,
    ags,
    agr,
    rss,
    rsr,
    ms,
    mr,
    zs,
    zr,
):
    dp = lax.axis_index("dp")
    tg = lax.axis_index("tensor")
    y, zl = dp // 4, dp % 4
    zh, x, c = tg // 8, (tg // 2) % 4, tg % 2
    z = zh * 4 + zl
    e = x * 2 + c

    def at(dy=0, dz=0, dx=0, dc=0):
        ny, nz, nx, nc = (y + dy + 4) % 4, (z + dz + 8) % 8, (x + dx + 4) % 4, (c + dc) % 2
        return (ny * 4 + nz % 4, (nz // 4) * 8 + nx * 2 + nc)

    def send(src, dst, ssem, rsem, dev):
        pltpu.make_async_remote_copy(
            src_ref=src,
            dst_ref=dst,
            send_sem=ssem,
            recv_sem=rsem,
            device_id=dev,
            device_id_type=MESH,
        ).start()

    def rows(z_, e_, half=None):
        if half is None:
            return X.at[:, pl.ds(pl.multiple_of(z_ * 256 + e_ * PART, PART), PART), :]
        return X.at[:, pl.ds(pl.multiple_of(z_ * 256 + e_ * PART + half * 16, 16), 16), :]

    own = pl.ds(pl.multiple_of(zl * 256, 256), 256)
    copies = [
        pltpu.make_async_copy(tok, X.at[0, own, :], loc.at[0]),
        pltpu.make_async_copy(cot, X.at[1, own, :], loc.at[1]),
        pltpu.make_async_copy(upk, wst.at[0], loc.at[2]),
        pltpu.make_async_copy(dnk, wst.at[1], loc.at[3]),
        pltpu.make_async_copy(fst, stg.at[pl.ds(0, 2)], loc.at[4]),
        pltpu.make_async_copy(snd, stg.at[pl.ds(2, 2)], loc.at[5]),
    ]
    for copy in copies:
        copy.start()

    copies[0].wait()
    copies[1].wait()
    send(rows(zl, e), rows(zl, e), t1s.at[0], t1r.at[0], at(dz=1))
    send(rows(zl, e), rows(zl, e), t1s.at[1], t1r.at[1], at(dz=-1))
    send(rows(zl, e, 0), rows(zl, e, 0), t1s.at[2], t1r.at[2], at(dz=2))
    send(rows(zl, e, 1), rows(zl, e, 1), t1s.at[3], t1r.at[3], at(dz=-2))

    line = lax.broadcasted_iota(jnp.int32, (ROWS, ROWS), 0)
    lane = lax.broadcasted_iota(jnp.int32, (ROWS, ROWS), 1)
    to_block = jnp.zeros((ROWS, ROWS), jnp.int32)
    from_block = jnp.zeros((ROWS, ROWS), jnp.int32)
    for k in range(N):
        here = (lane >> 4) == k
        to_block = jnp.where(here, bd[tg, k], to_block)
        from_block = jnp.where(here, (rank[k] + tg) & 15, from_block)
    within = (line & 15) == (lane & 15)
    order[...] = jnp.where(within & (to_block == (line >> 4)), 1.0, 0.0).astype(BF)
    pick[...] = jnp.where(within & (from_block == (line >> 4)), 1.0, 0.0).astype(BF)

    copies[2].wait()
    copies[3].wait()
    for m in range(2):
        sorted_rows = jnp.dot(order[...], wst[m], preferred_element_type=F32).astype(BF)
        mom[:, 4 + m] = sorted_rows.reshape(N, PIECE, WIDTH)
        wide = jnp.concatenate([sorted_rows, jnp.zeros((ROWS, 128), BF)], axis=1)
        for q in range(4):
            wq[:, q, m * PIECE : (m + 1) * PIECE, :] = wide[:, q * QUART : q * QUART + 256].reshape(
                N, PIECE, 256
            )

    me = z * 8 + e

    def send_weight(k, _):
        to = (me + k) % 64
        nz, nx, nc = to // 8, (to // 2) % 4, to % 2
        nt, nq = (nz // 4) * 8 + nx * 2 + nc, nz % 4
        send(wq.at[nt, nq], wr.at[zl * N + tg], wqs, wqr, (y * 4 + nq, nt))
        return 0

    lax.fori_loop(1, 64, send_weight, 0)
    own_block = pltpu.make_async_copy(wq.at[tg, zl], wr.at[zl * N + tg], loc.at[6])
    own_block.start()

    copies[4].wait()
    copies[5].wait()

    for k in range(4):
        sorted_rows = jnp.dot(order[...], stg[k].astype(BF), preferred_element_type=F32)
        mom[:, k] = sorted_rows.astype(BF).reshape(N, PIECE, WIDTH)

    came = [(zl + 3) % 4, (zl + 1) % 4, (zl + 2) % 4]
    for p in range(3):
        if p < 2:
            wait_bytes(rows(came[p], e), t1r.at[p])
        else:
            wait_bytes(rows(came[p], e, 0), t1r.at[2])
            wait_bytes(rows(came[p], e, 1), t1r.at[3])
        piece = rows(came[p], e)
        send(piece, piece, t2s.at[p, 0], t2r.at[p, 0], at(dx=1))
        send(piece, piece, t2s.at[p, 1], t2r.at[p, 1], at(dx=-1))
        send(piece, piece, t3s.at[p, 0], t3r.at[p, 0], at(dc=1))

    wait_bytes(wr.at[pl.ds(0, 63)], wqr)
    own_block.wait()

    def unpack(k, _):
        for m in range(2):
            block = wr[pl.ds(k * N, N), m * PIECE : (m + 1) * PIECE, :].reshape(ROWS, 256)
            turned = lax.dot_general(
                block, pick[...], (((0,), (1,)), ((), ())), preferred_element_type=F32
            )
            wall[y, m, :, pl.ds(pl.multiple_of(k * 256, 256), 256)] = turned[:QUART].astype(BF)
        return 0

    lax.fori_loop(0, 4, unpack, 0)
    send(wall.at[y], wall.at[y], ags.at[0], agr.at[0], at(dy=1))
    send(wall.at[y], wall.at[y], ags.at[1], agr.at[1], at(dy=-1))

    def send_moments(k, _):
        to = (tg + k) % N
        send(mom.at[to], momr.at[tg], ms, mr, (dp, to))
        return 0

    lax.fori_loop(1, N, send_moments, 0)
    own_moments = pltpu.make_async_copy(mom.at[tg], momr.at[tg], loc.at[7])
    own_moments.start()

    left, right, far = (x + 3) % 4 * 2 + c, (x + 1) % 4 * 2 + c, (x + 2) % 4 * 2 + c
    yl, yr, yf = (y + 3) % 4, (y + 1) % 4, (y + 2) % 4

    def pass_x(p):
        piece = rows(came[p], left)
        wait_bytes(piece, t2r.at[p, 0])
        half = rows(came[p], left, 0)
        send(half, half, t2s.at[p, 2], t2r.at[p, 2], at(dx=1))
        send(piece, piece, t3s.at[p, 1], t3r.at[p, 1], at(dc=1))
        piece = rows(came[p], right)
        wait_bytes(piece, t2r.at[p, 1])
        half = rows(came[p], right, 1)
        send(half, half, t2s.at[p, 3], t2r.at[p, 3], at(dx=-1))
        send(piece, piece, t3s.at[p, 2], t3r.at[p, 2], at(dc=1))

    pass_x(0)
    pass_x(1)
    wait_bytes(wall.at[yl], agr.at[0])
    send(wall.at[yl, 0], wall.at[yl, 0], ags.at[2], agr.at[2], at(dy=1))
    wait_bytes(wall.at[yr], agr.at[1])
    send(wall.at[yr, 1], wall.at[yr, 1], ags.at[3], agr.at[3], at(dy=-1))
    pass_x(2)
    for p in range(3):
        wait_bytes(rows(came[p], far, 0), t2r.at[p, 2])
        wait_bytes(rows(came[p], far, 1), t2r.at[p, 3])
        piece = rows(came[p], far)
        send(piece, piece, t3s.at[p, 3], t3r.at[p, 3], at(dc=1))
    for p in range(3):
        for k, dx in enumerate((0, 3, 1, 2)):
            wait_bytes(rows(came[p], (x + dx) % 4 * 2 + (1 - c)), t3r.at[p, k])
    wait_bytes(wall.at[yf, 0], agr.at[2])
    wait_bytes(wall.at[yf, 1], agr.at[3])

    acc[...] = jnp.zeros_like(acc)

    def forward(i, _):
        ny, k = i // 4, i % 4
        cols = pl.ds(pl.multiple_of(i * 256, 256), 256)
        part = pl.ds(pl.multiple_of(k * 256, 256), 256)
        for m in range(2):
            product = lax.dot_general(
                wall[ny, m, :, part],
                X[m, :, cols],
                (((1,), (1,)), ((), ())),
                preferred_element_type=F32,
            )
            acc[m] += product.astype(BF).astype(F32)
        return 0

    lax.fori_loop(0, N, forward, 0)

    def activate(i, _):
        cols = pl.ds(pl.multiple_of(i * 256, 256), 256)
        pre, back = acc[0, :, cols], acc[1, :, cols]
        sigma = jax.nn.sigmoid(pre)
        act[1, :, cols] = (pre * sigma).astype(BF)
        act[0, :, cols] = (back * sigma * (1.0 + pre * (1.0 - sigma))).astype(BF)
        return 0

    lax.fori_loop(0, 4, activate, 0)

    def gradient(ny):
        def step(i, _):
            cols = pl.ds(pl.multiple_of(ny * CHUNK + i * 256, 256), 256)
            part = pl.ds(pl.multiple_of(i * 256, 256), 256)
            for m in range(2):
                gp[ny, m, :, part] = jnp.dot(
                    act[m], X[m, :, cols], preferred_element_type=F32
                ).astype(BF)
            return 0

        lax.fori_loop(0, 4, step, 0)

    gradient(yf)
    send(gp.at[yf, 0], relay.at[0], rss.at[0], rsr.at[0], at(dy=1))
    send(gp.at[yf, 1], relay.at[1], rss.at[1], rsr.at[1], at(dy=-1))
    gradient(yr)
    send(gp.at[yr, 1], got.at[0, 1], rss.at[2], rsr.at[2], at(dy=1))
    gradient(yl)
    send(gp.at[yl, 0], got.at[1, 0], rss.at[3], rsr.at[3], at(dy=-1))
    gradient(y)
    wait_bytes(relay.at[0], rsr.at[0])
    gp[yr, 0] = (gp[yr, 0].astype(F32) + relay[0].astype(F32)).astype(BF)
    send(gp.at[yr, 0], got.at[0, 0], rss.at[4], rsr.at[4], at(dy=1))
    wait_bytes(relay.at[1], rsr.at[1])
    gp[yl, 1] = (gp[yl, 1].astype(F32) + relay[1].astype(F32)).astype(BF)
    send(gp.at[yl, 1], got.at[1, 1], rss.at[5], rsr.at[5], at(dy=-1))
    wait_bytes(got.at[0, 1], rsr.at[2])
    wait_bytes(got.at[1, 0], rsr.at[3])
    wait_bytes(got.at[0, 0], rsr.at[4])
    wait_bytes(got.at[1, 1], rsr.at[5])
    for m in range(2):
        gsum[m] = (
            gp[y, m].astype(F32) + got[0, m].astype(F32) + got[1, m].astype(F32)
        ).astype(BF)

    for k in range(1, 4):
        nq = (zl + k) % 4
        part = gsum.at[:, :, pl.ds(pl.multiple_of(nq * 256, 256), 256)]
        send(part, gout.at[zl], zs.at[k - 1], zr.at[k - 1], (y * 4 + nq, tg))
    own_part = pltpu.make_async_copy(
        gsum.at[:, :, pl.ds(pl.multiple_of(zl * 256, 256), 256)], gout.at[zl], loc.at[8]
    )
    own_part.start()

    wait_bytes(rows(zl, e), t1s.at[0])
    wait_bytes(rows(zl, e), t1s.at[1])
    wait_bytes(rows(zl, e, 0), t1s.at[2])
    wait_bytes(rows(zl, e, 1), t1s.at[3])
    for p in range(3):
        for k in range(4):
            wait_bytes(rows(zl, e, None if k < 2 else 0), t2s.at[p, k])
            wait_bytes(rows(zl, e), t3s.at[p, k])
    wait_bytes(wr.at[pl.ds(0, 63)], wqs)
    for k in range(2):
        wait_bytes(wall.at[y], ags.at[k])
        wait_bytes(wall.at[y, 0], ags.at[2 + k])
    for k in range(6):
        wait_bytes(gp.at[y, 0], rss.at[k])
    wait_bytes(mom.at[pl.ds(0, 15)], ms)
    wait_bytes(momr.at[pl.ds(0, 15)], mr)
    own_moments.wait()
    for k in range(3):
        wait_bytes(gout.at[k], zs.at[k])
        wait_bytes(gout.at[(zl + 3 - k) % 4], zr.at[k])
    own_part.wait()


def update(rank, momr, gin, new_up, new_dn, new_first, new_second, grad):
    step = pl.program_id(0)
    tg = lax.axis_index("tensor")

    @pl.when(step == 0)
    def _():
        for m in range(2):
            for q in range(2):
                lanes = pl.ds(q * 128, 128)
                tall = jnp.concatenate([gin[k, m, :, lanes].astype(F32) for k in range(4)], axis=0)
                grad[m, lanes, :] = tall.T

    for half in range(2):
        r = step * 2 + half
        src = jnp.int32(0)
        for k in range(N):
            src = src + jnp.where((rank[k] + tg) % N == r, k, 0)
        at_row = pl.ds(pl.multiple_of(r * PIECE, PIECE), PIECE)
        out_row = pl.ds(half * PIECE, PIECE)
        for m in range(2):
            g = grad[m, at_row, :]
            first = beta_first * momr[src, m].astype(F32) + (1.0 - beta_first) * g
            second = beta_second * momr[src, 2 + m].astype(F32) + (1.0 - beta_second) * g * g
            first_hat = first / (1.0 - beta_first**step_count)
            second_hat = second / (1.0 - beta_second**step_count)
            new = momr[src, 4 + m].astype(F32) - rate * first_hat / (jnp.sqrt(second_hat) + adam_eps)
            new_first[m, out_row, :] = first
            new_second[m, out_row, :] = second
            (new_up, new_dn)[m][out_row, :] = new.astype(BF)


def per_device(tok, cot, upk, dnk, fst, snd, bd, rank):
    anywhere = pl.BlockSpec(memory_space=pl.ANY)
    scalar = pl.BlockSpec(memory_space=pltpu.SMEM)
    dma = pltpu.SemaphoreType.DMA
    momr, gout = pl.pallas_call(
        exchange,
        out_shape=(
            jax.ShapeDtypeStruct((N, 6, PIECE, WIDTH), BF),
            jax.ShapeDtypeStruct((4, 2, QUART, 256), BF),
        ),
        in_specs=[scalar, scalar] + [anywhere] * 6,
        out_specs=(anywhere, anywhere),
        scratch_shapes=[
            pltpu.VMEM((2, TOK, D), BF),
            pltpu.VMEM((4, ROWS, WIDTH), F32),
            pltpu.VMEM((2, ROWS, WIDTH), BF),
            pltpu.VMEM((N, 4, 32, 256), BF),
            pltpu.VMEM((64, 32, 256), BF),
            pltpu.VMEM((N, 6, PIECE, WIDTH), BF),
            pltpu.VMEM((4, 2, QUART, CHUNK), BF),
            pltpu.VMEM((2, QUART, TOK), F32),
            pltpu.VMEM((2, QUART, TOK), BF),
            pltpu.VMEM((4, 2, QUART, CHUNK), BF),
            pltpu.VMEM((2, QUART, CHUNK), BF),
            pltpu.VMEM((2, 2, QUART, CHUNK), BF),
            pltpu.VMEM((2, QUART, CHUNK), BF),
            pltpu.VMEM((ROWS, ROWS), BF),
            pltpu.VMEM((ROWS, ROWS), BF),
            dma((9,)),
            dma((4,)),
            dma((4,)),
            dma((3, 4)),
            dma((3, 4)),
            dma((3, 4)),
            dma((3, 4)),
            dma,
            dma,
            dma((4,)),
            dma((4,)),
            dma((6,)),
            dma((6,)),
            dma,
            dma,
            dma((3,)),
            dma((3,)),
        ],
        compiler_params=pltpu.CompilerParams(
            has_side_effects=True, vmem_limit_bytes=60 * 2**20
        ),
        cost_estimate=pl.CostEstimate(
            flops=7_600_000_000, bytes_accessed=20_000_000, transcendentals=500_000
        ),
        name="exchange",
    )(bd, rank, tok, cot, upk, dnk, fst, snd)

    whole = pl.BlockSpec((N, 6, PIECE, WIDTH), lambda i: (0, 0, 0, 0))
    flat = pl.BlockSpec((32, WIDTH), lambda i: (i, 0))
    pair = pl.BlockSpec((2, 32, WIDTH), lambda i: (0, i, 0))
    return pl.pallas_call(
        update,
        grid=(8,),
        out_shape=(
            jax.ShapeDtypeStruct((ROWS, WIDTH), BF),
            jax.ShapeDtypeStruct((ROWS, WIDTH), BF),
            jax.ShapeDtypeStruct((2, ROWS, WIDTH), F32),
            jax.ShapeDtypeStruct((2, ROWS, WIDTH), F32),
        ),
        in_specs=[scalar, whole, pl.BlockSpec((4, 2, QUART, 256), lambda i: (0, 0, 0, 0))],
        out_specs=(flat, flat, pair, pair),
        scratch_shapes=[pltpu.VMEM((2, ROWS, WIDTH), F32)],
        compiler_params=pltpu.CompilerParams(vmem_limit_bytes=32 * 2**20),
        cost_estimate=pl.CostEstimate(
            flops=10_000_000, bytes_accessed=13_000_000, transcendentals=500_000
        ),
        name="update",
    )(rank, momr, gout)


def solution(mesh):
    in_specs = (
        P("dp", None),
        P("dp", None),
        P("dp", "tensor"),
        P("dp", "tensor"),
        P(None, "dp", "tensor"),
        P(None, "dp", "tensor"),
        P(),
        P(),
    )
    out_specs = (
        P("dp", "tensor"),
        P("dp", "tensor"),
        P(None, "dp", "tensor"),
        P(None, "dp", "tensor"),
    )
    return jax.shard_map(
        per_device, mesh=mesh, in_specs=in_specs, out_specs=out_specs, check_vma=False
    )
```

```python
import jax
import jax.numpy as jnp
from jax import lax
from jax.experimental import pallas as pl
from jax.experimental.pallas import tpu as pltpu
from jax.sharding import PartitionSpec as P

beta_first = 0.9
beta_second = 0.95
adam_eps = 1e-08
rate = 0.005
step_count = 20

MESH = pl.DeviceIdType.MESH
BF = jnp.bfloat16
F32 = jnp.float32

N = 16
PIECE = 16
ROWS = 256
WIDTH = 896
QUART = 224
HALF = 112
D = 4096
TOK = 1024
CHUNK = 1024
PART = 32


def wait_bytes(ref, sem):
    pltpu.make_async_copy(ref, ref, sem).wait()


def exchange(
    bd,
    rank,
    tok,
    cot,
    upk,
    dnk,
    fst,
    snd,
    momr,
    gout,
    X,
    stg,
    wst,
    wq,
    wr,
    mom,
    wall,
    acc,
    act,
    gp,
    relay,
    got,
    gsum,
    order,
    pick,
    row_in,
    pair_in,
    loc,
    t1s,
    t1r,
    t2s,
    t2r,
    t3s,
    t3r,
    wqs,
    wqr,
    ags,
    agr,
    rss,
    rsr,
    ms,
    mr,
    zs,
    zr,
):
    dp = lax.axis_index("dp")
    tg = lax.axis_index("tensor")
    y, zl = dp // 4, dp % 4
    zh, x, c = tg // 8, (tg // 2) % 4, tg % 2
    z = zh * 4 + zl
    e = x * 2 + c

    def at(dy=0, dz=0, dx=0, dc=0):
        ny, nz, nx, nc = (y + dy + 4) % 4, (z + dz + 8) % 8, (x + dx + 4) % 4, (c + dc) % 2
        return (ny * 4 + nz % 4, (nz // 4) * 8 + nx * 2 + nc)

    def send(src, dst, ssem, rsem, dev):
        pltpu.make_async_remote_copy(
            src_ref=src,
            dst_ref=dst,
            send_sem=ssem,
            recv_sem=rsem,
            device_id=dev,
            device_id_type=MESH,
        ).start()

    def rows(z_, e_, half=None):
        if half is None:
            return X.at[:, pl.ds(pl.multiple_of(z_ * 256 + e_ * PART, PART), PART), :]
        return X.at[:, pl.ds(pl.multiple_of(z_ * 256 + e_ * PART + half * 16, 16), 16), :]

    own = pl.ds(pl.multiple_of(zl * 256, 256), 256)
    copies = [
        pltpu.make_async_copy(tok, X.at[0, own, :], loc.at[0]),
        pltpu.make_async_copy(cot, X.at[1, own, :], loc.at[1]),
        pltpu.make_async_copy(upk, wst.at[0], loc.at[2]),
        pltpu.make_async_copy(dnk, wst.at[1], loc.at[3]),
        pltpu.make_async_copy(fst, stg.at[pl.ds(0, 2)], loc.at[4]),
        pltpu.make_async_copy(snd, stg.at[pl.ds(2, 2)], loc.at[5]),
    ]
    for copy in copies:
        copy.start()

    barrier = pltpu.get_barrier_semaphore()

    def greet(sem, dev):
        pl.semaphore_signal(sem, inc=1, device_id=dev, device_id_type=MESH)

    for k in range(1, 8):
        greet(barrier, at(dz=k))
    for k in range(1, 4):
        greet(barrier, at(dx=k))
    greet(barrier, at(dc=1))
    greet(barrier, at(dy=1))
    greet(barrier, at(dy=-1))
    pl.semaphore_wait(barrier, 13)
    for k in range(1, 4):
        greet(row_in, at(dx=k))

    copies[0].wait()
    copies[1].wait()
    for k in range(2):
        send(rows(zl, e, k), rows(zl, e, k), t1s.at[k], t1r.at[k], at(dz=1))
        send(rows(zl, e, 1 - k), rows(zl, e, 1 - k), t1s.at[2 + k], t1r.at[2 + k], at(dz=-1))

    line = lax.broadcasted_iota(jnp.int32, (ROWS, ROWS), 0)
    lane = lax.broadcasted_iota(jnp.int32, (ROWS, ROWS), 1)
    to_block = jnp.zeros((ROWS, ROWS), jnp.int32)
    from_block = jnp.zeros((ROWS, ROWS), jnp.int32)
    for k in range(N):
        here = (lane >> 4) == k
        to_block = jnp.where(here, bd[tg, k], to_block)
        from_block = jnp.where(here, (rank[k] + tg) & 15, from_block)
    within = (line & 15) == (lane & 15)
    order[...] = jnp.where(within & (to_block == (line >> 4)), 1.0, 0.0).astype(BF)
    pick[...] = jnp.where(within & (from_block == (line >> 4)), 1.0, 0.0).astype(BF)

    copies[2].wait()
    copies[3].wait()
    for m in range(2):
        sorted_rows = jnp.dot(order[...], wst[m], preferred_element_type=F32).astype(BF)
        mom[:, 4 + m] = sorted_rows.reshape(N, PIECE, WIDTH)
        wide = jnp.concatenate([sorted_rows, jnp.zeros((ROWS, 128), BF)], axis=1)
        for q in range(4):
            for h in range(2):
                first = q * QUART + h * HALF
                wq[:, q, h, m * PIECE : (m + 1) * PIECE, :] = wide[:, first : first + 128].reshape(
                    N, PIECE, 128
                )

    pl.semaphore_wait(row_in, 3)
    greet(pair_in, at(dc=1))

    copies[4].wait()
    copies[5].wait()
    for k in range(4):
        sorted_rows = jnp.dot(order[...], stg[k].astype(BF), preferred_element_type=F32)
        mom[:, k] = sorted_rows.astype(BF).reshape(N, PIECE, WIDTH)

    def send_moments(dzh, dx, dc):
        to = (zh + dzh) % 2 * 8 + (x + dx) % 4 * 2 + (c + dc) % 2
        send(mom.at[to], momr.at[tg], ms, mr, (dp, to))

    pl.semaphore_wait(pair_in, 1)

    def same_half(k, _):
        send_moments(0, k // 2, k % 2)
        return 0

    lax.fori_loop(1, 8, same_half, 0)
    own_moments = pltpu.make_async_copy(mom.at[tg], momr.at[tg], loc.at[7])
    own_moments.start()

    came = [(zl + 3) % 4, (zl + 1) % 4, (zl + 2) % 4]

    def spread(p, k):
        half = rows(came[p], e, k)
        send(half, half, t2s.at[p, k], t2r.at[p, k], at(dx=1))
        send(half, half, t2s.at[p, 2 + k], t2r.at[p, 2 + k], at(dx=-1))

    def spread_core(p):
        piece = rows(came[p], e)
        send(piece, piece, t3s.at[p, 0], t3r.at[p, 0], at(dc=1))

    half = rows(came[0], e, 0)
    wait_bytes(half, t1r.at[0])
    send(half, half, t1s.at[4], t1r.at[4], at(dz=1))
    spread(0, 0)
    half = rows(came[1], e, 1)
    wait_bytes(half, t1r.at[2])
    send(half, half, t1s.at[5], t1r.at[5], at(dz=-1))
    spread(1, 1)
    wait_bytes(rows(came[0], e, 1), t1r.at[1])
    spread(0, 1)
    wait_bytes(rows(came[1], e, 0), t1r.at[3])
    spread(1, 0)

    me = z * 8 + e

    def send_weights(h):
        def step(k, _):
            to = (me + k) % 64
            nz, nx, nc = to // 8, (to // 2) % 4, to % 2
            nt, nq = (nz // 4) * 8 + nx * 2 + nc, nz % 4
            send(wq.at[nt, nq, h], wr.at[h, zl * N + tg], wqs.at[h], wqr.at[h], (y * 4 + nq, nt))
            return 0

        lax.fori_loop(1, 64, step, 0)
        own_block = pltpu.make_async_copy(wq.at[tg, zl, h], wr.at[h, zl * N + tg], loc.at[10 + h])
        own_block.start()
        return own_block

    own_blocks = [send_weights(0), send_weights(1)]
    spread_core(0)
    spread_core(1)

    wait_bytes(rows(came[2], e, 0), t1r.at[4])
    spread(2, 0)
    wait_bytes(rows(came[2], e, 1), t1r.at[5])
    spread(2, 1)
    spread_core(2)

    for h in range(2):
        wait_bytes(wr.at[h, pl.ds(0, 63)], wqr.at[h])
        own_blocks[h].wait()

        def unpack(k, _, h=h):
            for m in range(2):
                block = wr[h, pl.ds(k * N, N), m * PIECE : (m + 1) * PIECE, :].reshape(ROWS, 128)
                turned = lax.dot_general(
                    block, pick[...], (((0,), (1,)), ((), ())), preferred_element_type=F32
                )
                part = pl.ds(pl.multiple_of(k * 256, 256), 256)
                wall[h, y, m, :, part] = turned[:HALF].astype(BF)
            return 0

        lax.fori_loop(0, 4, unpack, 0)
        send(wall.at[h, y], wall.at[h, y], ags.at[h, 0], agr.at[h, 0], at(dy=1))
        send(wall.at[h, y], wall.at[h, y], ags.at[h, 1], agr.at[h, 1], at(dy=-1))

    lax.fori_loop(0, 2, lambda k, _: (send_moments(1, 0, k), 0)[1], 0)

    def near_half(k, _):
        send_moments(1, 1 + k // 2 * 2, k % 2)
        return 0

    left, right, far = (x + 3) % 4 * 2 + c, (x + 1) % 4 * 2 + c, (x + 2) % 4 * 2 + c
    yl, yr, yf = (y + 3) % 4, (y + 1) % 4, (y + 2) % 4

    def pass_x(p):
        half = rows(came[p], left, 0)
        wait_bytes(half, t2r.at[p, 0])
        send(half, half, t2s.at[p, 4], t2r.at[p, 4], at(dx=1))
        half = rows(came[p], right, 1)
        wait_bytes(half, t2r.at[p, 3])
        send(half, half, t2s.at[p, 5], t2r.at[p, 5], at(dx=-1))
        wait_bytes(rows(came[p], left, 1), t2r.at[p, 1])
        piece = rows(came[p], left)
        send(piece, piece, t3s.at[p, 1], t3r.at[p, 1], at(dc=1))
        wait_bytes(rows(came[p], right, 0), t2r.at[p, 2])
        piece = rows(came[p], right)
        send(piece, piece, t3s.at[p, 2], t3r.at[p, 2], at(dc=1))

    def pass_y(h):
        wait_bytes(wall.at[h, yl], agr.at[h, 0])
        send(wall.at[h, yl, 0], wall.at[h, yl, 0], ags.at[h, 2], agr.at[h, 2], at(dy=1))
        wait_bytes(wall.at[h, yr], agr.at[h, 1])
        send(wall.at[h, yr, 1], wall.at[h, yr, 1], ags.at[h, 3], agr.at[h, 3], at(dy=-1))

    def end_x(p):
        wait_bytes(rows(came[p], far, 0), t2r.at[p, 4])
        wait_bytes(rows(came[p], far, 1), t2r.at[p, 5])
        piece = rows(came[p], far)
        send(piece, piece, t3s.at[p, 3], t3r.at[p, 3], at(dc=1))

    def end_tokens(p):
        for k, dx in enumerate((0, 3, 1, 2)):
            wait_bytes(rows(came[p], (x + dx) % 4 * 2 + (1 - c)), t3r.at[p, k])

    def end_y(h):
        wait_bytes(wall.at[h, yf, 0], agr.at[h, 2])
        wait_bytes(wall.at[h, yf, 1], agr.at[h, 3])

    def forward(nz):
        seen = pl.ds(pl.multiple_of(nz * 256, 256), 256)

        def step(ny, _):
            for m in range(2):
                total = jnp.zeros((QUART, 256), F32)
                for k in range(4):
                    cols = pl.ds(pl.multiple_of(ny * CHUNK + k * 256, 256), 256)
                    part = pl.ds(k * 256, 256)
                    weight = jnp.concatenate(
                        [wall[0, ny, m, :, part], wall[1, ny, m, :, part]], axis=0
                    )
                    product = lax.dot_general(
                        weight,
                        X[m, seen, cols],
                        (((1,), (1,)), ((), ())),
                        preferred_element_type=F32,
                    )
                    total += product.astype(BF).astype(F32)
                acc[m] += total
            return 0

        acc[...] = jnp.zeros_like(acc)
        lax.fori_loop(0, 4, step, 0)
        pre, back = acc[0], acc[1]
        sigma = jax.nn.sigmoid(pre)
        act[1, :, seen] = (pre * sigma).astype(BF)
        act[0, :, seen] = (back * sigma * (1.0 + pre * (1.0 - sigma))).astype(BF)

    upper, lower = pl.ds(0, HALF), pl.ds(HALF, HALF)

    def gradient(m, ny):
        def step(i, _):
            cols = pl.ds(pl.multiple_of(ny * CHUNK + i * 256, 256), 256)
            part = pl.ds(pl.multiple_of(i * 256, 256), 256)
            gp[m, ny, :, part] = jnp.dot(
                act[m], X[m, :, cols], preferred_element_type=F32
            ).astype(BF)
            return 0

        lax.fori_loop(0, 4, step, 0)

    def gradients(m):
        gradient(m, yf)
        send(gp.at[m, yf, upper], relay.at[m, 0], rss.at[m, 0], rsr.at[m, 0], at(dy=1))
        send(gp.at[m, yf, lower], relay.at[m, 1], rss.at[m, 1], rsr.at[m, 1], at(dy=-1))
        gradient(m, yr)
        send(gp.at[m, yr, lower], got.at[m, 0, lower], rss.at[m, 2], rsr.at[m, 2], at(dy=1))
        gradient(m, yl)
        send(gp.at[m, yl, upper], got.at[m, 1, upper], rss.at[m, 3], rsr.at[m, 3], at(dy=-1))
        gradient(m, y)

    def relays(m):
        wait_bytes(relay.at[m, 0], rsr.at[m, 0])
        gp[m, yr, upper] = (gp[m, yr, upper].astype(F32) + relay[m, 0].astype(F32)).astype(BF)
        send(gp.at[m, yr, upper], got.at[m, 0, upper], rss.at[m, 4], rsr.at[m, 4], at(dy=1))
        wait_bytes(relay.at[m, 1], rsr.at[m, 1])
        gp[m, yl, lower] = (gp[m, yl, lower].astype(F32) + relay[m, 1].astype(F32)).astype(BF)
        send(gp.at[m, yl, lower], got.at[m, 1, lower], rss.at[m, 5], rsr.at[m, 5], at(dy=-1))

    own_parts = []

    def finish(m):
        wait_bytes(got.at[m, 0, lower], rsr.at[m, 2])
        wait_bytes(got.at[m, 1, upper], rsr.at[m, 3])
        wait_bytes(got.at[m, 0, upper], rsr.at[m, 4])
        wait_bytes(got.at[m, 1, lower], rsr.at[m, 5])
        gsum[m] = (
            gp[m, y].astype(F32) + got[m, 0].astype(F32) + got[m, 1].astype(F32)
        ).astype(BF)
        for k in range(1, 4):
            nq = (zl + k) % 4
            part = gsum.at[m, :, pl.ds(pl.multiple_of(nq * 256, 256), 256)]
            send(part, gout.at[m, zl], zs.at[m, k - 1], zr.at[m, k - 1], (y * 4 + nq, tg))
        own_part = pltpu.make_async_copy(
            gsum.at[m, :, pl.ds(pl.multiple_of(zl * 256, 256), 256)], gout.at[m, zl], loc.at[8 + m]
        )
        own_part.start()
        own_parts.append(own_part)

    pass_x(0)
    pass_x(1)
    pass_y(0)
    pass_x(2)
    lax.fori_loop(0, 4, near_half, 0)
    pass_y(1)
    for p in range(3):
        end_x(p)
    lax.fori_loop(0, 2, lambda k, _: (send_moments(1, 2, k), 0)[1], 0)
    end_y(0)
    end_y(1)
    forward(zl)
    for p in range(3):
        end_tokens(p)
        forward(came[p])
    gradients(0)
    gradients(1)
    relays(0)
    relays(1)
    finish(0)
    finish(1)

    for k in range(6):
        wait_bytes(rows(zl, e, 0), t1s.at[k])
    for p in range(3):
        for k in range(6):
            wait_bytes(rows(zl, e, 0), t2s.at[p, k])
        for k in range(4):
            wait_bytes(rows(zl, e), t3s.at[p, k])
    for h in range(2):
        wait_bytes(wr.at[h, pl.ds(0, 63)], wqs.at[h])
    for h in range(2):
        for k in range(2):
            wait_bytes(wall.at[h, y], ags.at[h, k])
            wait_bytes(wall.at[h, y, 0], ags.at[h, 2 + k])
        for k in range(6):
            wait_bytes(gp.at[h, y, upper], rss.at[h, k])
        for k in range(3):
            wait_bytes(gout.at[h, k], zs.at[h, k])
            wait_bytes(gout.at[h, (zl + 3 - k) % 4], zr.at[h, k])
        own_parts[h].wait()
    wait_bytes(mom.at[pl.ds(0, 15)], ms)
    wait_bytes(momr.at[pl.ds(0, 15)], mr)
    own_moments.wait()


def update(rank, momr, gin, new_up, new_dn, new_first, new_second, grad):
    step = pl.program_id(0)
    tg = lax.axis_index("tensor")

    @pl.when(step == 0)
    def _():
        for m in range(2):
            for q in range(2):
                lanes = pl.ds(q * 128, 128)
                tall = jnp.concatenate([
                    gin[m, k, :, lanes].astype(F32) for k in range(4)
                ], axis=0)
                grad[m, lanes, :] = tall.T

    for half in range(2):
        r = step * 2 + half
        src = jnp.int32(0)
        for k in range(N):
            src = src + jnp.where((rank[k] + tg) % N == r, k, 0)
        at_row = pl.ds(pl.multiple_of(r * PIECE, PIECE), PIECE)
        out_row = pl.ds(half * PIECE, PIECE)
        for m in range(2):
            g = grad[m, at_row, :]
            first = beta_first * momr[src, m].astype(F32) + (1.0 - beta_first) * g
            second = beta_second * momr[src, 2 + m].astype(F32) + (1.0 - beta_second) * g * g
            first_hat = first / (1.0 - beta_first**step_count)
            second_hat = second / (1.0 - beta_second**step_count)
            new = momr[src, 4 + m].astype(F32) - rate * first_hat / (jnp.sqrt(second_hat) + adam_eps)
            new_first[m, out_row, :] = first
            new_second[m, out_row, :] = second
            (new_up, new_dn)[m][out_row, :] = new.astype(BF)


def per_device(tok, cot, upk, dnk, fst, snd, bd, rank):
    anywhere = pl.BlockSpec(memory_space=pl.ANY)
    scalar = pl.BlockSpec(memory_space=pltpu.SMEM)
    dma = pltpu.SemaphoreType.DMA
    momr, gout = pl.pallas_call(
        exchange,
        out_shape=(
            jax.ShapeDtypeStruct((N, 6, PIECE, WIDTH), BF),
            jax.ShapeDtypeStruct((2, 4, QUART, 256), BF),
        ),
        in_specs=[scalar, scalar] + [anywhere] * 6,
        out_specs=(anywhere, anywhere),
        scratch_shapes=[
            pltpu.VMEM((2, TOK, D), BF),
            pltpu.VMEM((4, ROWS, WIDTH), F32),
            pltpu.VMEM((2, ROWS, WIDTH), BF),
            pltpu.VMEM((N, 4, 2, 32, 128), BF),
            pltpu.VMEM((2, 64, 32, 128), BF),
            pltpu.VMEM((N, 6, PIECE, WIDTH), BF),
            pltpu.VMEM((2, 4, 2, HALF, CHUNK), BF),
            pltpu.VMEM((2, QUART, 256), F32),
            pltpu.VMEM((2, QUART, TOK), BF),
            pltpu.VMEM((2, 4, QUART, CHUNK), BF),
            pltpu.VMEM((2, 2, HALF, CHUNK), BF),
            pltpu.VMEM((2, 2, QUART, CHUNK), BF),
            pltpu.VMEM((2, QUART, CHUNK), BF),
            pltpu.VMEM((ROWS, ROWS), BF),
            pltpu.VMEM((ROWS, ROWS), BF),
            pltpu.SemaphoreType.REGULAR,
            pltpu.SemaphoreType.REGULAR,
            dma((12,)),
            dma((6,)),
            dma((6,)),
            dma((3, 6)),
            dma((3, 6)),
            dma((3, 4)),
            dma((3, 4)),
            dma((2,)),
            dma((2,)),
            dma((2, 4)),
            dma((2, 4)),
            dma((2, 6)),
            dma((2, 6)),
            dma,
            dma,
            dma((2, 3)),
            dma((2, 3)),
        ],
        compiler_params=pltpu.CompilerParams(
            has_side_effects=True, collective_id=0, vmem_limit_bytes=60 * 2**20
        ),
        cost_estimate=pl.CostEstimate(
            flops=7_600_000_000, bytes_accessed=20_000_000, transcendentals=500_000
        ),
        name="exchange",
    )(bd, rank, tok, cot, upk, dnk, fst, snd)

    whole = pl.BlockSpec((N, 6, PIECE, WIDTH), lambda i: (0, 0, 0, 0))
    flat = pl.BlockSpec((32, WIDTH), lambda i: (i, 0))
    pair = pl.BlockSpec((2, 32, WIDTH), lambda i: (0, i, 0))
    return pl.pallas_call(
        update,
        grid=(8,),
        out_shape=(
            jax.ShapeDtypeStruct((ROWS, WIDTH), BF),
            jax.ShapeDtypeStruct((ROWS, WIDTH), BF),
            jax.ShapeDtypeStruct((2, ROWS, WIDTH), F32),
            jax.ShapeDtypeStruct((2, ROWS, WIDTH), F32),
        ),
        in_specs=[scalar, whole, pl.BlockSpec((2, 4, QUART, 256), lambda i: (0,) * 4)],
        out_specs=(flat, flat, pair, pair),
        scratch_shapes=[pltpu.VMEM((2, ROWS, WIDTH), F32)],
        compiler_params=pltpu.CompilerParams(vmem_limit_bytes=32 * 2**20),
        cost_estimate=pl.CostEstimate(
            flops=10_000_000, bytes_accessed=13_000_000, transcendentals=500_000
        ),
        name="update",
    )(rank, momr, gout)


def solution(mesh):
    in_specs = (
        P("dp", None),
        P("dp", None),
        P("dp", "tensor"),
        P("dp", "tensor"),
        P(None, "dp", "tensor"),
        P(None, "dp", "tensor"),
        P(),
        P(),
    )
    out_specs = (
        P("dp", "tensor"),
        P("dp", "tensor"),
        P(None, "dp", "tensor"),
        P(None, "dp", "tensor"),
    )
    return jax.shard_map(
        per_device, mesh=mesh, in_specs=in_specs, out_specs=out_specs, check_vma=False
    )
```

```python
import jax
import jax.numpy as jnp
from jax import lax
from jax.experimental import pallas as pl
from jax.experimental.pallas import tpu as pltpu
from jax.sharding import PartitionSpec as P

beta_first = 0.9
beta_second = 0.95
adam_eps = 1e-08
rate = 0.005
step_count = 20

MESH = pl.DeviceIdType.MESH
BF = jnp.bfloat16
F32 = jnp.float32

N = 16
PIECE = 16
ROWS = 256
WIDTH = 896
QUART = 224
HALF = 112
D = 4096
TOK = 1024
CHUNK = 1024
PART = 32


def wait_bytes(ref, sem):
    pltpu.make_async_copy(ref, ref, sem).wait()


def exchange(
    bd,
    rank,
    tok,
    cot,
    upk,
    dnk,
    fst,
    snd,
    momr,
    gout,
    X,
    stg,
    wst,
    wq,
    wr,
    mom,
    wall,
    acc,
    act,
    gp,
    relay,
    got,
    gsum,
    order,
    pick,
    row_in,
    pair_in,
    loc,
    t1s,
    t1r,
    t2s,
    t2r,
    t3s,
    t3r,
    wqs,
    wqr,
    ags,
    agr,
    rss,
    rsr,
    ms,
    mr,
    zs,
    zr,
):
    dp = lax.axis_index("dp")
    tg = lax.axis_index("tensor")
    y, zl = dp // 4, dp % 4
    zh, x, c = tg // 8, (tg // 2) % 4, tg % 2
    z = zh * 4 + zl
    e = x * 2 + c

    def at(dy=0, dz=0, dx=0, dc=0):
        ny, nz, nx, nc = (y + dy + 4) % 4, (z + dz + 8) % 8, (x + dx + 4) % 4, (c + dc) % 2
        return (ny * 4 + nz % 4, (nz // 4) * 8 + nx * 2 + nc)

    def send(src, dst, ssem, rsem, dev):
        pltpu.make_async_remote_copy(
            src_ref=src,
            dst_ref=dst,
            send_sem=ssem,
            recv_sem=rsem,
            device_id=dev,
            device_id_type=MESH,
        ).start()

    def rows(z_, e_, half=None):
        if half is None:
            return X.at[:, pl.ds(pl.multiple_of(z_ * 256 + e_ * PART, PART), PART), :]
        return X.at[:, pl.ds(pl.multiple_of(z_ * 256 + e_ * PART + half * 16, 16), 16), :]

    own = pl.ds(pl.multiple_of(zl * 256, 256), 256)
    copies = [
        pltpu.make_async_copy(tok, X.at[0, own, :], loc.at[0]),
        pltpu.make_async_copy(cot, X.at[1, own, :], loc.at[1]),
        pltpu.make_async_copy(upk, wst.at[0], loc.at[2]),
        pltpu.make_async_copy(dnk, wst.at[1], loc.at[3]),
        pltpu.make_async_copy(fst, stg.at[pl.ds(0, 2)], loc.at[4]),
        pltpu.make_async_copy(snd, stg.at[pl.ds(2, 2)], loc.at[5]),
    ]
    for copy in copies:
        copy.start()

    barrier = pltpu.get_barrier_semaphore()

    def greet(sem, dev):
        pl.semaphore_signal(sem, inc=1, device_id=dev, device_id_type=MESH)

    for k in range(1, 8):
        greet(barrier, at(dz=k))
    for k in range(1, 4):
        greet(barrier, at(dx=k))
    greet(barrier, at(dc=1))
    greet(barrier, at(dy=1))
    greet(barrier, at(dy=-1))
    pl.semaphore_wait(barrier, 13)
    for k in range(1, 4):
        greet(row_in, at(dx=k))

    copies[0].wait()
    copies[1].wait()
    for k in range(2):
        send(rows(zl, e, k), rows(zl, e, k), t1s.at[k], t1r.at[k], at(dz=1))
        send(rows(zl, e, 1 - k), rows(zl, e, 1 - k), t1s.at[2 + k], t1r.at[2 + k], at(dz=-1))

    line = lax.broadcasted_iota(jnp.int32, (ROWS, ROWS), 0)
    lane = lax.broadcasted_iota(jnp.int32, (ROWS, ROWS), 1)
    to_block = jnp.zeros((ROWS, ROWS), jnp.int32)
    from_block = jnp.zeros((ROWS, ROWS), jnp.int32)
    for k in range(N):
        here = (lane >> 4) == k
        to_block = jnp.where(here, bd[tg, k], to_block)
        from_block = jnp.where(here, (rank[k] + tg) & 15, from_block)
    within = (line & 15) == (lane & 15)
    order[...] = jnp.where(within & (to_block == (line >> 4)), 1.0, 0.0).astype(BF)
    pick[...] = jnp.where(within & (from_block == (line >> 4)), 1.0, 0.0).astype(BF)

    copies[2].wait()
    copies[3].wait()
    for m in range(2):
        sorted_rows = jnp.dot(order[...], wst[m], preferred_element_type=F32).astype(BF)
        mom[:, 4 + m] = sorted_rows.reshape(N, PIECE, WIDTH)
        wide = jnp.concatenate([sorted_rows, jnp.zeros((ROWS, 128), BF)], axis=1)
        for q in range(4):
            for h in range(2):
                first = q * QUART + h * HALF
                wq[:, q, h, m * PIECE : (m + 1) * PIECE, :] = wide[:, first : first + 128].reshape(
                    N, PIECE, 128
                )

    pl.semaphore_wait(row_in, 3)
    greet(pair_in, at(dc=1))
    pl.semaphore_wait(pair_in, 1)

    me = z * 8 + e

    def send_weights(h):
        def step(k, _):
            to = (me + k) % 64
            nz, nx, nc = to // 8, (to // 2) % 4, to % 2
            nt, nq = (nz // 4) * 8 + nx * 2 + nc, nz % 4
            send(wq.at[nt, nq, h], wr.at[h, zl * N + tg], wqs.at[h], wqr.at[h], (y * 4 + nq, nt))
            return 0

        lax.fori_loop(1, 64, step, 0)
        own_block = pltpu.make_async_copy(wq.at[tg, zl, h], wr.at[h, zl * N + tg], loc.at[10 + h])
        own_block.start()
        return own_block

    own_blocks = [send_weights(0), send_weights(1)]

    came = [(zl + 3) % 4, (zl + 1) % 4, (zl + 2) % 4]

    def spread(p, k):
        half = rows(came[p], e, k)
        send(half, half, t2s.at[p, k], t2r.at[p, k], at(dx=1))
        send(half, half, t2s.at[p, 2 + k], t2r.at[p, 2 + k], at(dx=-1))

    def spread_core(p):
        piece = rows(came[p], e)
        send(piece, piece, t3s.at[p, 0], t3r.at[p, 0], at(dc=1))

    half = rows(came[0], e, 0)
    wait_bytes(half, t1r.at[0])
    send(half, half, t1s.at[4], t1r.at[4], at(dz=1))
    spread(0, 0)
    half = rows(came[1], e, 1)
    wait_bytes(half, t1r.at[2])
    send(half, half, t1s.at[5], t1r.at[5], at(dz=-1))
    spread(1, 1)
    wait_bytes(rows(came[0], e, 1), t1r.at[1])
    spread(0, 1)
    wait_bytes(rows(came[1], e, 0), t1r.at[3])
    spread(1, 0)

    spread_core(0)
    spread_core(1)

    copies[4].wait()
    copies[5].wait()
    for k in range(4):
        sorted_rows = jnp.dot(order[...], stg[k].astype(BF), preferred_element_type=F32)
        mom[:, k] = sorted_rows.astype(BF).reshape(N, PIECE, WIDTH)

    def send_moments(dzh, dx, dc):
        to = (zh + dzh) % 2 * 8 + (x + dx) % 4 * 2 + (c + dc) % 2
        send(mom.at[to], momr.at[tg], ms, mr, (dp, to))

    own_moments = pltpu.make_async_copy(mom.at[tg], momr.at[tg], loc.at[7])
    own_moments.start()


    wait_bytes(rows(came[2], e, 0), t1r.at[4])
    spread(2, 0)
    wait_bytes(rows(came[2], e, 1), t1r.at[5])
    spread(2, 1)
    spread_core(2)

    for h in range(2):
        wait_bytes(wr.at[h, pl.ds(0, 63)], wqr.at[h])
        own_blocks[h].wait()

        def unpack(k, _, h=h):
            for m in range(2):
                block = wr[h, pl.ds(k * N, N), m * PIECE : (m + 1) * PIECE, :].reshape(ROWS, 128)
                turned = lax.dot_general(
                    block, pick[...], (((0,), (1,)), ((), ())), preferred_element_type=F32
                )
                part = pl.ds(pl.multiple_of(k * 256, 256), 256)
                wall[h, y, m, :, part] = turned[:HALF].astype(BF)
            return 0

        lax.fori_loop(0, 4, unpack, 0)
        send(wall.at[h, y], wall.at[h, y], ags.at[h, 0], agr.at[h, 0], at(dy=1))
        send(wall.at[h, y], wall.at[h, y], ags.at[h, 1], agr.at[h, 1], at(dy=-1))

    lax.fori_loop(0, 2, lambda k, _: (send_moments(1, 0, k), 0)[1], 0)

    def near_half(k, _):
        send_moments(1, 1 + k // 2 * 2, k % 2)
        return 0

    left, right, far = (x + 3) % 4 * 2 + c, (x + 1) % 4 * 2 + c, (x + 2) % 4 * 2 + c
    yl, yr, yf = (y + 3) % 4, (y + 1) % 4, (y + 2) % 4

    def pass_x(p):
        half = rows(came[p], left, 0)
        wait_bytes(half, t2r.at[p, 0])
        send(half, half, t2s.at[p, 4], t2r.at[p, 4], at(dx=1))
        half = rows(came[p], right, 1)
        wait_bytes(half, t2r.at[p, 3])
        send(half, half, t2s.at[p, 5], t2r.at[p, 5], at(dx=-1))
        wait_bytes(rows(came[p], left, 1), t2r.at[p, 1])
        piece = rows(came[p], left)
        send(piece, piece, t3s.at[p, 1], t3r.at[p, 1], at(dc=1))
        wait_bytes(rows(came[p], right, 0), t2r.at[p, 2])
        piece = rows(came[p], right)
        send(piece, piece, t3s.at[p, 2], t3r.at[p, 2], at(dc=1))

    def pass_y(h):
        wait_bytes(wall.at[h, yl], agr.at[h, 0])
        send(wall.at[h, yl, 0], wall.at[h, yl, 0], ags.at[h, 2], agr.at[h, 2], at(dy=1))
        wait_bytes(wall.at[h, yr], agr.at[h, 1])
        send(wall.at[h, yr, 1], wall.at[h, yr, 1], ags.at[h, 3], agr.at[h, 3], at(dy=-1))

    def end_x(p):
        wait_bytes(rows(came[p], far, 0), t2r.at[p, 4])
        wait_bytes(rows(came[p], far, 1), t2r.at[p, 5])
        piece = rows(came[p], far)
        send(piece, piece, t3s.at[p, 3], t3r.at[p, 3], at(dc=1))

    def end_tokens(p):
        for k, dx in enumerate((0, 3, 1, 2)):
            wait_bytes(rows(came[p], (x + dx) % 4 * 2 + (1 - c)), t3r.at[p, k])

    def end_y(h):
        wait_bytes(wall.at[h, yf, 0], agr.at[h, 2])
        wait_bytes(wall.at[h, yf, 1], agr.at[h, 3])

    def forward(nz):
        seen = pl.ds(pl.multiple_of(nz * 256, 256), 256)

        def step(ny, _):
            for m in range(2):
                total = jnp.zeros((QUART, 256), F32)
                for k in range(4):
                    cols = pl.ds(pl.multiple_of(ny * CHUNK + k * 256, 256), 256)
                    part = pl.ds(k * 256, 256)
                    weight = jnp.concatenate(
                        [wall[0, ny, m, :, part], wall[1, ny, m, :, part]], axis=0
                    )
                    product = lax.dot_general(
                        weight,
                        X[m, seen, cols],
                        (((1,), (1,)), ((), ())),
                        preferred_element_type=F32,
                    )
                    total += product.astype(BF).astype(F32)
                acc[m] += total
            return 0

        acc[...] = jnp.zeros_like(acc)
        lax.fori_loop(0, 4, step, 0)
        pre, back = acc[0], acc[1]
        sigma = jax.nn.sigmoid(pre)
        act[1, :, seen] = (pre * sigma).astype(BF)
        act[0, :, seen] = (back * sigma * (1.0 + pre * (1.0 - sigma))).astype(BF)

    upper, lower = pl.ds(0, HALF), pl.ds(HALF, HALF)

    def gradient(m, ny):
        def step(i, _):
            cols = pl.ds(pl.multiple_of(ny * CHUNK + i * 256, 256), 256)
            part = pl.ds(pl.multiple_of(i * 256, 256), 256)
            gp[m, ny, :, part] = jnp.dot(
                act[m], X[m, :, cols], preferred_element_type=F32
            ).astype(BF)
            return 0

        lax.fori_loop(0, 4, step, 0)

    def far_gradient(m):
        gradient(m, yf)
        send(gp.at[m, yf, upper], relay.at[m, 0], rss.at[m, 0], rsr.at[m, 0], at(dy=1))
        send(gp.at[m, yf, lower], relay.at[m, 1], rss.at[m, 1], rsr.at[m, 1], at(dy=-1))

    def near_gradients(m):
        gradient(m, yr)
        send(gp.at[m, yr, lower], got.at[m, 0, lower], rss.at[m, 2], rsr.at[m, 2], at(dy=1))
        gradient(m, yl)
        send(gp.at[m, yl, upper], got.at[m, 1, upper], rss.at[m, 3], rsr.at[m, 3], at(dy=-1))

    def relays(m):
        wait_bytes(relay.at[m, 0], rsr.at[m, 0])
        gp[m, yr, upper] = (gp[m, yr, upper].astype(F32) + relay[m, 0].astype(F32)).astype(BF)
        send(gp.at[m, yr, upper], got.at[m, 0, upper], rss.at[m, 4], rsr.at[m, 4], at(dy=1))
        wait_bytes(relay.at[m, 1], rsr.at[m, 1])
        gp[m, yl, lower] = (gp[m, yl, lower].astype(F32) + relay[m, 1].astype(F32)).astype(BF)
        send(gp.at[m, yl, lower], got.at[m, 1, lower], rss.at[m, 5], rsr.at[m, 5], at(dy=-1))

    own_parts = []

    def finish(m):
        wait_bytes(got.at[m, 0, lower], rsr.at[m, 2])
        wait_bytes(got.at[m, 1, upper], rsr.at[m, 3])
        wait_bytes(got.at[m, 0, upper], rsr.at[m, 4])
        wait_bytes(got.at[m, 1, lower], rsr.at[m, 5])
        gsum[m] = (
            gp[m, y].astype(F32) + got[m, 0].astype(F32) + got[m, 1].astype(F32)
        ).astype(BF)
        for k in range(1, 4):
            nq = (zl + k) % 4
            part = gsum.at[m, :, pl.ds(pl.multiple_of(nq * 256, 256), 256)]
            send(part, gout.at[m, zl], zs.at[m, k - 1], zr.at[m, k - 1], (y * 4 + nq, tg))
        own_part = pltpu.make_async_copy(
            gsum.at[m, :, pl.ds(pl.multiple_of(zl * 256, 256), 256)], gout.at[m, zl], loc.at[8 + m]
        )
        own_part.start()
        own_parts.append(own_part)

    pass_x(0)
    pass_x(1)
    pass_y(0)
    pass_x(2)
    lax.fori_loop(0, 4, near_half, 0)
    pass_y(1)
    end_y(0)
    end_y(1)
    forward(zl)
    end_x(0)
    end_x(1)
    end_tokens(0)
    forward(came[0])
    end_x(2)
    lax.fori_loop(0, 2, lambda k, _: (send_moments(1, 2, k), 0)[1], 0)
    for k in range(1, 8):
        send_moments(0, k // 2, k % 2)
    end_tokens(1)
    forward(came[1])
    end_tokens(2)
    forward(came[2])
    far_gradient(0)
    near_gradients(0)
    far_gradient(1)
    relays(0)
    near_gradients(1)
    gradient(0, y)
    gradient(1, y)
    relays(1)
    finish(0)
    finish(1)

    for k in range(6):
        wait_bytes(rows(zl, e, 0), t1s.at[k])
    for p in range(3):
        for k in range(6):
            wait_bytes(rows(zl, e, 0), t2s.at[p, k])
        for k in range(4):
            wait_bytes(rows(zl, e), t3s.at[p, k])
    for h in range(2):
        wait_bytes(wr.at[h, pl.ds(0, 63)], wqs.at[h])
    for h in range(2):
        for k in range(2):
            wait_bytes(wall.at[h, y], ags.at[h, k])
            wait_bytes(wall.at[h, y, 0], ags.at[h, 2 + k])
        for k in range(6):
            wait_bytes(gp.at[h, y, upper], rss.at[h, k])
        for k in range(3):
            wait_bytes(gout.at[h, k], zs.at[h, k])
            wait_bytes(gout.at[h, (zl + 3 - k) % 4], zr.at[h, k])
        own_parts[h].wait()
    wait_bytes(mom.at[pl.ds(0, 15)], ms)
    wait_bytes(momr.at[pl.ds(0, 15)], mr)
    own_moments.wait()


def update(rank, momr, gin, new_up, new_dn, new_first, new_second, grad):
    step = pl.program_id(0)
    tg = lax.axis_index("tensor")

    @pl.when(step == 0)
    def _():
        for m in range(2):
            for q in range(2):
                lanes = pl.ds(q * 128, 128)
                tall = jnp.concatenate([
                    gin[m, k, :, lanes].astype(F32) for k in range(4)
                ], axis=0)
                grad[m, lanes, :] = tall.T

    for half in range(2):
        r = step * 2 + half
        src = jnp.int32(0)
        for k in range(N):
            src = src + jnp.where((rank[k] + tg) % N == r, k, 0)
        at_row = pl.ds(pl.multiple_of(r * PIECE, PIECE), PIECE)
        out_row = pl.ds(half * PIECE, PIECE)
        for m in range(2):
            g = grad[m, at_row, :]
            first = beta_first * momr[src, m].astype(F32) + (1.0 - beta_first) * g
            second = beta_second * momr[src, 2 + m].astype(F32) + (1.0 - beta_second) * g * g
            first_hat = first / (1.0 - beta_first**step_count)
            second_hat = second / (1.0 - beta_second**step_count)
            new = momr[src, 4 + m].astype(F32) - rate * first_hat / (jnp.sqrt(second_hat) + adam_eps)
            new_first[m, out_row, :] = first
            new_second[m, out_row, :] = second
            (new_up, new_dn)[m][out_row, :] = new.astype(BF)


def per_device(tok, cot, upk, dnk, fst, snd, bd, rank):
    anywhere = pl.BlockSpec(memory_space=pl.ANY)
    scalar = pl.BlockSpec(memory_space=pltpu.SMEM)
    dma = pltpu.SemaphoreType.DMA
    momr, gout = pl.pallas_call(
        exchange,
        out_shape=(
            jax.ShapeDtypeStruct((N, 6, PIECE, WIDTH), BF),
            jax.ShapeDtypeStruct((2, 4, QUART, 256), BF),
        ),
        in_specs=[scalar, scalar] + [anywhere] * 6,
        out_specs=(anywhere, anywhere),
        scratch_shapes=[
            pltpu.VMEM((2, TOK, D), BF),
            pltpu.VMEM((4, ROWS, WIDTH), F32),
            pltpu.VMEM((2, ROWS, WIDTH), BF),
            pltpu.VMEM((N, 4, 2, 32, 128), BF),
            pltpu.VMEM((2, 64, 32, 128), BF),
            pltpu.VMEM((N, 6, PIECE, WIDTH), BF),
            pltpu.VMEM((2, 4, 2, HALF, CHUNK), BF),
            pltpu.VMEM((2, QUART, 256), F32),
            pltpu.VMEM((2, QUART, TOK), BF),
            pltpu.VMEM((2, 4, QUART, CHUNK), BF),
            pltpu.VMEM((2, 2, HALF, CHUNK), BF),
            pltpu.VMEM((2, 2, QUART, CHUNK), BF),
            pltpu.VMEM((2, QUART, CHUNK), BF),
            pltpu.VMEM((ROWS, ROWS), BF),
            pltpu.VMEM((ROWS, ROWS), BF),
            pltpu.SemaphoreType.REGULAR,
            pltpu.SemaphoreType.REGULAR,
            dma((12,)),
            dma((6,)),
            dma((6,)),
            dma((3, 6)),
            dma((3, 6)),
            dma((3, 4)),
            dma((3, 4)),
            dma((2,)),
            dma((2,)),
            dma((2, 4)),
            dma((2, 4)),
            dma((2, 6)),
            dma((2, 6)),
            dma,
            dma,
            dma((2, 3)),
            dma((2, 3)),
        ],
        compiler_params=pltpu.CompilerParams(
            has_side_effects=True, collective_id=0, vmem_limit_bytes=60 * 2**20
        ),
        cost_estimate=pl.CostEstimate(
            flops=7_600_000_000, bytes_accessed=20_000_000, transcendentals=500_000
        ),
        name="exchange",
    )(bd, rank, tok, cot, upk, dnk, fst, snd)

    whole = pl.BlockSpec((N, 6, PIECE, WIDTH), lambda i: (0, 0, 0, 0))
    flat = pl.BlockSpec((32, WIDTH), lambda i: (i, 0))
    pair = pl.BlockSpec((2, 32, WIDTH), lambda i: (0, i, 0))
    return pl.pallas_call(
        update,
        grid=(8,),
        out_shape=(
            jax.ShapeDtypeStruct((ROWS, WIDTH), BF),
            jax.ShapeDtypeStruct((ROWS, WIDTH), BF),
            jax.ShapeDtypeStruct((2, ROWS, WIDTH), F32),
            jax.ShapeDtypeStruct((2, ROWS, WIDTH), F32),
        ),
        in_specs=[scalar, whole, pl.BlockSpec((2, 4, QUART, 256), lambda i: (0,) * 4)],
        out_specs=(flat, flat, pair, pair),
        scratch_shapes=[pltpu.VMEM((2, ROWS, WIDTH), F32)],
        compiler_params=pltpu.CompilerParams(vmem_limit_bytes=60 * 2**20),
        cost_estimate=pl.CostEstimate(
            flops=10_000_000, bytes_accessed=13_000_000, transcendentals=500_000
        ),
        name="update",
    )(rank, momr, gout)


def solution(mesh):
    in_specs = (
        P("dp", None),
        P("dp", None),
        P("dp", "tensor"),
        P("dp", "tensor"),
        P(None, "dp", "tensor"),
        P(None, "dp", "tensor"),
        P(),
        P(),
    )
    out_specs = (
        P("dp", "tensor"),
        P("dp", "tensor"),
        P(None, "dp", "tensor"),
        P(None, "dp", "tensor"),
    )
    return jax.shard_map(
        per_device, mesh=mesh, in_specs=in_specs, out_specs=out_specs, check_vma=False
    )
```

```python
import jax
import jax.numpy as jnp
from jax import lax
from jax.experimental import pallas as pl
from jax.experimental.pallas import tpu as pltpu
from jax.sharding import PartitionSpec as P

beta_first = 0.9
beta_second = 0.95
adam_eps = 1e-08
rate = 0.005
step_count = 20

MESH = pl.DeviceIdType.MESH
BF = jnp.bfloat16
F32 = jnp.float32

N = 16
PIECE = 16
ROWS = 256
WIDTH = 896
QUART = 224
HALF = 112
D = 4096
TOK = 1024
CHUNK = 1024
PART = 32


def wait_bytes(ref, sem):
    pltpu.make_async_copy(ref, ref, sem).wait()


def exchange(
    bd,
    rank,
    tok,
    cot,
    upk,
    dnk,
    fst,
    snd,
    momr,
    gout,
    X,
    stg,
    wst,
    wq,
    wr,
    mom,
    wall,
    acc,
    act,
    gp,
    relay,
    got,
    gsum,
    order,
    pick,
    row_in,
    pair_in,
    loc,
    t1s,
    t1r,
    t2s,
    t2r,
    t3s,
    t3r,
    wqs,
    wqr,
    ags,
    agr,
    rss,
    rsr,
    ms,
    mr,
    zs,
    zr,
):
    dp = lax.axis_index("dp")
    tg = lax.axis_index("tensor")
    y, zl = dp // 4, dp % 4
    zh, x, c = tg // 8, (tg // 2) % 4, tg % 2
    z = zh * 4 + zl
    e = x * 2 + c

    def at(dy=0, dz=0, dx=0, dc=0):
        ny, nz, nx, nc = (y + dy + 4) % 4, (z + dz + 8) % 8, (x + dx + 4) % 4, (c + dc) % 2
        return (ny * 4 + nz % 4, (nz // 4) * 8 + nx * 2 + nc)

    def send(src, dst, ssem, rsem, dev):
        pltpu.make_async_remote_copy(
            src_ref=src,
            dst_ref=dst,
            send_sem=ssem,
            recv_sem=rsem,
            device_id=dev,
            device_id_type=MESH,
        ).start()

    def rows(z_, e_, half=None):
        if half is None:
            return X.at[:, pl.ds(pl.multiple_of(z_ * 256 + e_ * PART, PART), PART), :]
        return X.at[:, pl.ds(pl.multiple_of(z_ * 256 + e_ * PART + half * 16, 16), 16), :]

    own = pl.ds(pl.multiple_of(zl * 256, 256), 256)
    copies = [
        pltpu.make_async_copy(tok, X.at[0, own, :], loc.at[0]),
        pltpu.make_async_copy(cot, X.at[1, own, :], loc.at[1]),
        pltpu.make_async_copy(upk, wst.at[0], loc.at[2]),
        pltpu.make_async_copy(dnk, wst.at[1], loc.at[3]),
        pltpu.make_async_copy(fst, stg.at[pl.ds(0, 2)], loc.at[4]),
        pltpu.make_async_copy(snd, stg.at[pl.ds(2, 2)], loc.at[5]),
    ]
    for copy in copies:
        copy.start()

    barrier = pltpu.get_barrier_semaphore()

    def greet(sem, dev):
        pl.semaphore_signal(sem, inc=1, device_id=dev, device_id_type=MESH)

    for k in range(1, 8):
        greet(barrier, at(dz=k))
    for k in range(1, 4):
        greet(barrier, at(dx=k))
    greet(barrier, at(dc=1))
    greet(barrier, at(dy=1))
    greet(barrier, at(dy=-1))
    pl.semaphore_wait(barrier, 13)
    for k in range(1, 4):
        greet(row_in, at(dx=k))

    copies[0].wait()
    copies[1].wait()
    for k in range(2):
        send(rows(zl, e, k), rows(zl, e, k), t1s.at[k], t1r.at[k], at(dz=1))
        send(rows(zl, e, 1 - k), rows(zl, e, 1 - k), t1s.at[2 + k], t1r.at[2 + k], at(dz=-1))

    line = lax.broadcasted_iota(jnp.int32, (ROWS, ROWS), 0)
    lane = lax.broadcasted_iota(jnp.int32, (ROWS, ROWS), 1)
    to_block = jnp.zeros((ROWS, ROWS), jnp.int32)
    from_block = jnp.zeros((ROWS, ROWS), jnp.int32)
    for k in range(N):
        here = (lane >> 4) == k
        to_block = jnp.where(here, bd[tg, k], to_block)
        from_block = jnp.where(here, (rank[k] + tg) & 15, from_block)
    within = (line & 15) == (lane & 15)
    order[...] = jnp.where(within & (to_block == (line >> 4)), 1.0, 0.0).astype(BF)
    pick[...] = jnp.where(within & (from_block == (line >> 4)), 1.0, 0.0).astype(BF)

    copies[2].wait()
    copies[3].wait()
    for m in range(2):
        sorted_rows = jnp.dot(order[...], wst[m], preferred_element_type=F32).astype(BF)
        mom[:, 4 + m] = sorted_rows.reshape(N, PIECE, WIDTH)
        wide = jnp.concatenate([sorted_rows, jnp.zeros((ROWS, 128), BF)], axis=1)
        for q in range(4):
            for h in range(2):
                first = q * QUART + h * HALF
                wq[:, q, h, m * PIECE : (m + 1) * PIECE, :] = wide[:, first : first + 128].reshape(
                    N, PIECE, 128
                )

    pl.semaphore_wait(row_in, 3)
    greet(pair_in, at(dc=1))
    pl.semaphore_wait(pair_in, 1)

    me = z * 8 + e

    def send_weights(h):
        def step(k, _):
            to = (me + k) % 64
            nz, nx, nc = to // 8, (to // 2) % 4, to % 2
            nt, nq = (nz // 4) * 8 + nx * 2 + nc, nz % 4
            send(wq.at[nt, nq, h], wr.at[h, zl * N + tg], wqs.at[h], wqr.at[h], (y * 4 + nq, nt))
            return 0

        lax.fori_loop(1, 64, step, 0)
        own_block = pltpu.make_async_copy(wq.at[tg, zl, h], wr.at[h, zl * N + tg], loc.at[10 + h])
        own_block.start()
        return own_block

    own_blocks = [send_weights(0), send_weights(1)]

    came = [(zl + 3) % 4, (zl + 1) % 4, (zl + 2) % 4]

    def spread(p, k):
        half = rows(came[p], e, k)
        send(half, half, t2s.at[p, k], t2r.at[p, k], at(dx=1))
        send(half, half, t2s.at[p, 2 + k], t2r.at[p, 2 + k], at(dx=-1))

    def spread_core(p):
        piece = rows(came[p], e)
        send(piece, piece, t3s.at[p, 0], t3r.at[p, 0], at(dc=1))

    half = rows(came[0], e, 0)
    wait_bytes(half, t1r.at[0])
    send(half, half, t1s.at[4], t1r.at[4], at(dz=1))
    spread(0, 0)
    half = rows(came[1], e, 1)
    wait_bytes(half, t1r.at[2])
    send(half, half, t1s.at[5], t1r.at[5], at(dz=-1))
    spread(1, 1)
    wait_bytes(rows(came[0], e, 1), t1r.at[1])
    spread(0, 1)
    wait_bytes(rows(came[1], e, 0), t1r.at[3])
    spread(1, 0)

    spread_core(0)
    spread_core(1)

    copies[4].wait()
    copies[5].wait()
    for k in range(4):
        sorted_rows = jnp.dot(order[...], stg[k].astype(BF), preferred_element_type=F32)
        mom[:, k] = sorted_rows.astype(BF).reshape(N, PIECE, WIDTH)

    def send_moments(dzh, dx, dc):
        to = (zh + dzh) % 2 * 8 + (x + dx) % 4 * 2 + (c + dc) % 2
        send(mom.at[to], momr.at[tg], ms, mr, (dp, to))

    own_moments = pltpu.make_async_copy(mom.at[tg], momr.at[tg], loc.at[7])
    own_moments.start()


    wait_bytes(rows(came[2], e, 0), t1r.at[4])
    spread(2, 0)
    wait_bytes(rows(came[2], e, 1), t1r.at[5])
    spread(2, 1)
    spread_core(2)

    for h in range(2):
        wait_bytes(wr.at[h, pl.ds(0, 63)], wqr.at[h])
        own_blocks[h].wait()

        def unpack(k, _, h=h):
            for m in range(2):
                block = wr[h, pl.ds(k * N, N), m * PIECE : (m + 1) * PIECE, :].reshape(ROWS, 128)
                turned = lax.dot_general(
                    block, pick[...], (((0,), (1,)), ((), ())), preferred_element_type=F32
                )
                part = pl.ds(pl.multiple_of(k * 256, 256), 256)
                wall[h, y, m, :, part] = turned[:HALF].astype(BF)
            return 0

        lax.fori_loop(0, 4, unpack, 0)
        send(wall.at[h, y], wall.at[h, y], ags.at[h, 0], agr.at[h, 0], at(dy=1))
        send(wall.at[h, y], wall.at[h, y], ags.at[h, 1], agr.at[h, 1], at(dy=-1))

    lax.fori_loop(0, 2, lambda k, _: (send_moments(1, 0, k), 0)[1], 0)

    def near_half(k, _):
        send_moments(1, 1 + k // 2 * 2, k % 2)
        return 0

    left, right, far = (x + 3) % 4 * 2 + c, (x + 1) % 4 * 2 + c, (x + 2) % 4 * 2 + c
    yl, yr, yf = (y + 3) % 4, (y + 1) % 4, (y + 2) % 4

    def pass_x(p):
        half = rows(came[p], left, 0)
        wait_bytes(half, t2r.at[p, 0])
        send(half, half, t2s.at[p, 4], t2r.at[p, 4], at(dx=1))
        half = rows(came[p], right, 1)
        wait_bytes(half, t2r.at[p, 3])
        send(half, half, t2s.at[p, 5], t2r.at[p, 5], at(dx=-1))
        wait_bytes(rows(came[p], left, 1), t2r.at[p, 1])
        piece = rows(came[p], left)
        send(piece, piece, t3s.at[p, 1], t3r.at[p, 1], at(dc=1))
        wait_bytes(rows(came[p], right, 0), t2r.at[p, 2])
        piece = rows(came[p], right)
        send(piece, piece, t3s.at[p, 2], t3r.at[p, 2], at(dc=1))

    def pass_y(h):
        wait_bytes(wall.at[h, yl], agr.at[h, 0])
        send(wall.at[h, yl, 0], wall.at[h, yl, 0], ags.at[h, 2], agr.at[h, 2], at(dy=1))
        wait_bytes(wall.at[h, yr], agr.at[h, 1])
        send(wall.at[h, yr, 1], wall.at[h, yr, 1], ags.at[h, 3], agr.at[h, 3], at(dy=-1))

    def end_x(p):
        wait_bytes(rows(came[p], far, 0), t2r.at[p, 4])
        wait_bytes(rows(came[p], far, 1), t2r.at[p, 5])
        piece = rows(came[p], far)
        send(piece, piece, t3s.at[p, 3], t3r.at[p, 3], at(dc=1))

    def end_tokens(p):
        for k, dx in enumerate((0, 3, 1, 2)):
            wait_bytes(rows(came[p], (x + dx) % 4 * 2 + (1 - c)), t3r.at[p, k])

    def end_y(h):
        wait_bytes(wall.at[h, yf, 0], agr.at[h, 2])
        wait_bytes(wall.at[h, yf, 1], agr.at[h, 3])

    def forward(nz):
        seen = pl.ds(pl.multiple_of(nz * 256, 256), 256)

        def step(ny, _):
            for m in range(2):
                total = jnp.zeros((QUART, 256), F32)
                for k in range(4):
                    cols = pl.ds(pl.multiple_of(ny * CHUNK + k * 256, 256), 256)
                    part = pl.ds(k * 256, 256)
                    weight = jnp.concatenate(
                        [wall[0, ny, m, :, part], wall[1, ny, m, :, part]], axis=0
                    )
                    product = lax.dot_general(
                        weight,
                        X[m, seen, cols],
                        (((1,), (1,)), ((), ())),
                        preferred_element_type=F32,
                    )
                    total += product.astype(BF).astype(F32)
                acc[m] += total
            return 0

        acc[...] = jnp.zeros_like(acc)
        lax.fori_loop(0, 4, step, 0)
        pre, back = acc[0], acc[1]
        sigma = jax.nn.sigmoid(pre)
        act[1, :, seen] = (pre * sigma).astype(BF)
        act[0, :, seen] = (back * sigma * (1.0 + pre * (1.0 - sigma))).astype(BF)

    upper, lower = pl.ds(0, HALF), pl.ds(HALF, HALF)

    def gradient(m, ny):
        def step(i, _):
            cols = pl.ds(pl.multiple_of(ny * CHUNK + i * 256, 256), 256)
            part = pl.ds(pl.multiple_of(i * 256, 256), 256)
            gp[m, ny, :, part] = jnp.dot(
                act[m], X[m, :, cols], preferred_element_type=F32
            ).astype(BF)
            return 0

        lax.fori_loop(0, 4, step, 0)

    def far_gradient(m):
        gradient(m, yf)
        send(gp.at[m, yf, upper], relay.at[m, 0], rss.at[m, 0], rsr.at[m, 0], at(dy=1))
        send(gp.at[m, yf, lower], relay.at[m, 1], rss.at[m, 1], rsr.at[m, 1], at(dy=-1))

    def near_gradients(m):
        gradient(m, yr)
        send(gp.at[m, yr, lower], got.at[m, 0, lower], rss.at[m, 2], rsr.at[m, 2], at(dy=1))
        gradient(m, yl)
        send(gp.at[m, yl, upper], got.at[m, 1, upper], rss.at[m, 3], rsr.at[m, 3], at(dy=-1))

    def relays(m):
        wait_bytes(relay.at[m, 0], rsr.at[m, 0])
        gp[m, yr, upper] = (gp[m, yr, upper].astype(F32) + relay[m, 0].astype(F32)).astype(BF)
        send(gp.at[m, yr, upper], got.at[m, 0, upper], rss.at[m, 4], rsr.at[m, 4], at(dy=1))
        wait_bytes(relay.at[m, 1], rsr.at[m, 1])
        gp[m, yl, lower] = (gp[m, yl, lower].astype(F32) + relay[m, 1].astype(F32)).astype(BF)
        send(gp.at[m, yl, lower], got.at[m, 1, lower], rss.at[m, 5], rsr.at[m, 5], at(dy=-1))

    own_parts = []

    def finish(m):
        wait_bytes(got.at[m, 0, lower], rsr.at[m, 2])
        wait_bytes(got.at[m, 1, upper], rsr.at[m, 3])
        wait_bytes(got.at[m, 0, upper], rsr.at[m, 4])
        wait_bytes(got.at[m, 1, lower], rsr.at[m, 5])
        gsum[m] = (
            gp[m, y].astype(F32) + got[m, 0].astype(F32) + got[m, 1].astype(F32)
        ).astype(BF)
        for k in range(1, 4):
            nq = (zl + k) % 4
            part = gsum.at[m, :, pl.ds(pl.multiple_of(nq * 256, 256), 256)]
            send(part, gout.at[m, zl], zs.at[m, k - 1], zr.at[m, k - 1], (y * 4 + nq, tg))
        own_part = pltpu.make_async_copy(
            gsum.at[m, :, pl.ds(pl.multiple_of(zl * 256, 256), 256)], gout.at[m, zl], loc.at[8 + m]
        )
        own_part.start()
        own_parts.append(own_part)

    pass_x(0)
    pass_x(1)
    pass_y(0)
    pass_x(2)
    lax.fori_loop(0, 4, near_half, 0)
    pass_y(1)
    end_y(0)
    end_y(1)
    forward(zl)
    end_x(0)
    end_x(1)
    end_tokens(0)
    forward(came[0])
    end_x(2)
    lax.fori_loop(0, 2, lambda k, _: (send_moments(1, 2, k), 0)[1], 0)
    for k in range(1, 8):
        send_moments(0, k // 2, k % 2)
    end_tokens(1)
    forward(came[1])
    end_tokens(2)
    forward(came[2])
    far_gradient(0)
    near_gradients(0)
    far_gradient(1)
    relays(0)
    near_gradients(1)
    gradient(0, y)
    gradient(1, y)
    relays(1)
    finish(0)
    finish(1)

    for k in range(6):
        wait_bytes(rows(zl, e, 0), t1s.at[k])
    for p in range(3):
        for k in range(6):
            wait_bytes(rows(zl, e, 0), t2s.at[p, k])
        for k in range(4):
            wait_bytes(rows(zl, e), t3s.at[p, k])
    for h in range(2):
        wait_bytes(wr.at[h, pl.ds(0, 63)], wqs.at[h])
    for h in range(2):
        for k in range(2):
            wait_bytes(wall.at[h, y], ags.at[h, k])
            wait_bytes(wall.at[h, y, 0], ags.at[h, 2 + k])
        for k in range(6):
            wait_bytes(gp.at[h, y, upper], rss.at[h, k])
        for k in range(3):
            wait_bytes(gout.at[h, k], zs.at[h, k])
            wait_bytes(gout.at[h, (zl + 3 - k) % 4], zr.at[h, k])
        own_parts[h].wait()
    wait_bytes(mom.at[pl.ds(0, 15)], ms)
    wait_bytes(momr.at[pl.ds(0, 15)], mr)
    own_moments.wait()


def update(rank, momr, gin, new_up, new_dn, new_first, new_second, grad):
    step = pl.program_id(0)
    tg = lax.axis_index("tensor")

    @pl.when(step == 0)
    def _():
        for m in range(2):
            for q in range(2):
                lanes = pl.ds(q * 128, 128)
                tall = jnp.concatenate([
                    gin[m, k, :, lanes].astype(F32) for k in range(4)
                ], axis=0)
                grad[m, lanes, :] = tall.T

    for half in range(4):
        r = step * 4 + half
        src = jnp.int32(0)
        for k in range(N):
            src = src + jnp.where((rank[k] + tg) % N == r, k, 0)
        at_row = pl.ds(pl.multiple_of(r * PIECE, PIECE), PIECE)
        out_row = pl.ds(half * PIECE, PIECE)
        for m in range(2):
            g = grad[m, at_row, :]
            first = beta_first * momr[src, m].astype(F32) + (1.0 - beta_first) * g
            second = beta_second * momr[src, 2 + m].astype(F32) + (1.0 - beta_second) * g * g
            first_hat = first / (1.0 - beta_first**step_count)
            second_hat = second / (1.0 - beta_second**step_count)
            new = momr[src, 4 + m].astype(F32) - rate * first_hat / (jnp.sqrt(second_hat) + adam_eps)
            new_first[m, out_row, :] = first
            new_second[m, out_row, :] = second
            (new_up, new_dn)[m][out_row, :] = new.astype(BF)


def per_device(tok, cot, upk, dnk, fst, snd, bd, rank):
    anywhere = pl.BlockSpec(memory_space=pl.ANY)
    scalar = pl.BlockSpec(memory_space=pltpu.SMEM)
    dma = pltpu.SemaphoreType.DMA
    momr, gout = pl.pallas_call(
        exchange,
        out_shape=(
            jax.ShapeDtypeStruct((N, 6, PIECE, WIDTH), BF),
            jax.ShapeDtypeStruct((2, 4, QUART, 256), BF),
        ),
        in_specs=[scalar, scalar] + [anywhere] * 6,
        out_specs=(anywhere, anywhere),
        scratch_shapes=[
            pltpu.VMEM((2, TOK, D), BF),
            pltpu.VMEM((4, ROWS, WIDTH), F32),
            pltpu.VMEM((2, ROWS, WIDTH), BF),
            pltpu.VMEM((N, 4, 2, 32, 128), BF),
            pltpu.VMEM((2, 64, 32, 128), BF),
            pltpu.VMEM((N, 6, PIECE, WIDTH), BF),
            pltpu.VMEM((2, 4, 2, HALF, CHUNK), BF),
            pltpu.VMEM((2, QUART, 256), F32),
            pltpu.VMEM((2, QUART, TOK), BF),
            pltpu.VMEM((2, 4, QUART, CHUNK), BF),
            pltpu.VMEM((2, 2, HALF, CHUNK), BF),
            pltpu.VMEM((2, 2, QUART, CHUNK), BF),
            pltpu.VMEM((2, QUART, CHUNK), BF),
            pltpu.VMEM((ROWS, ROWS), BF),
            pltpu.VMEM((ROWS, ROWS), BF),
            pltpu.SemaphoreType.REGULAR,
            pltpu.SemaphoreType.REGULAR,
            dma((12,)),
            dma((6,)),
            dma((6,)),
            dma((3, 6)),
            dma((3, 6)),
            dma((3, 4)),
            dma((3, 4)),
            dma((2,)),
            dma((2,)),
            dma((2, 4)),
            dma((2, 4)),
            dma((2, 6)),
            dma((2, 6)),
            dma,
            dma,
            dma((2, 3)),
            dma((2, 3)),
        ],
        compiler_params=pltpu.CompilerParams(
            has_side_effects=True, collective_id=0, vmem_limit_bytes=60 * 2**20
        ),
        cost_estimate=pl.CostEstimate(
            flops=7_600_000_000, bytes_accessed=20_000_000, transcendentals=500_000
        ),
        name="exchange",
    )(bd, rank, tok, cot, upk, dnk, fst, snd)

    whole = pl.BlockSpec((N, 6, PIECE, WIDTH), lambda i: (0, 0, 0, 0))
    flat = pl.BlockSpec((64, WIDTH), lambda i: (i, 0))
    pair = pl.BlockSpec((2, 64, WIDTH), lambda i: (0, i, 0))
    return pl.pallas_call(
        update,
        grid=(4,),
        out_shape=(
            jax.ShapeDtypeStruct((ROWS, WIDTH), BF),
            jax.ShapeDtypeStruct((ROWS, WIDTH), BF),
            jax.ShapeDtypeStruct((2, ROWS, WIDTH), F32),
            jax.ShapeDtypeStruct((2, ROWS, WIDTH), F32),
        ),
        in_specs=[scalar, whole, pl.BlockSpec((2, 4, QUART, 256), lambda i: (0,) * 4)],
        out_specs=(flat, flat, pair, pair),
        scratch_shapes=[pltpu.VMEM((2, ROWS, WIDTH), F32)],
        compiler_params=pltpu.CompilerParams(vmem_limit_bytes=60 * 2**20),
        cost_estimate=pl.CostEstimate(
            flops=10_000_000, bytes_accessed=13_000_000, transcendentals=500_000
        ),
        name="update",
    )(rank, momr, gout)


def solution(mesh):
    in_specs = (
        P("dp", None),
        P("dp", None),
        P("dp", "tensor"),
        P("dp", "tensor"),
        P(None, "dp", "tensor"),
        P(None, "dp", "tensor"),
        P(),
        P(),
    )
    out_specs = (
        P("dp", "tensor"),
        P("dp", "tensor"),
        P(None, "dp", "tensor"),
        P(None, "dp", "tensor"),
    )
    return jax.shard_map(
        per_device, mesh=mesh, in_specs=in_specs, out_specs=out_specs, check_vma=False
    )
```

```python
import jax
import jax.numpy as jnp
from jax import lax
from jax.experimental import pallas as pl
from jax.experimental.pallas import tpu as pltpu
from jax.sharding import PartitionSpec as P

beta_first = 0.9
beta_second = 0.95
adam_eps = 1e-08
rate = 0.005
step_count = 20

MESH = pl.DeviceIdType.MESH
BF = jnp.bfloat16
F32 = jnp.float32

N = 16
PIECE = 16
ROWS = 256
WIDTH = 896
QUART = 224
HALF = 112
D = 4096
TOK = 1024
CHUNK = 1024
PART = 32


def wait_bytes(ref, sem):
    pltpu.make_async_copy(ref, ref, sem).wait()


def exchange(
    bd,
    rank,
    tok,
    cot,
    upk,
    dnk,
    fst,
    snd,
    momr,
    gout,
    X,
    stg,
    wst,
    wq,
    wr,
    mom,
    wall,
    acc,
    act,
    gp,
    relay,
    got,
    gsum,
    order,
    pick,
    row_in,
    pair_in,
    loc,
    t1s,
    t1r,
    t2s,
    t2r,
    t3s,
    t3r,
    wqs,
    wqr,
    ags,
    agr,
    rss,
    rsr,
    ms,
    mr,
    zs,
    zr,
):
    dp = lax.axis_index("dp")
    tg = lax.axis_index("tensor")
    y, zl = dp // 4, dp % 4
    zh, x, c = tg // 8, (tg // 2) % 4, tg % 2
    z = zh * 4 + zl
    e = x * 2 + c

    def at(dy=0, dz=0, dx=0, dc=0):
        ny, nz, nx, nc = (y + dy + 4) % 4, (z + dz + 8) % 8, (x + dx + 4) % 4, (c + dc) % 2
        return (ny * 4 + nz % 4, (nz // 4) * 8 + nx * 2 + nc)

    def send(src, dst, ssem, rsem, dev):
        pltpu.make_async_remote_copy(
            src_ref=src,
            dst_ref=dst,
            send_sem=ssem,
            recv_sem=rsem,
            device_id=dev,
            device_id_type=MESH,
        ).start()

    def rows(z_, e_, half=None):
        if half is None:
            return X.at[:, pl.ds(pl.multiple_of(z_ * 256 + e_ * PART, PART), PART), :]
        return X.at[:, pl.ds(pl.multiple_of(z_ * 256 + e_ * PART + half * 16, 16), 16), :]

    own = pl.ds(pl.multiple_of(zl * 256, 256), 256)
    copies = [
        pltpu.make_async_copy(tok, X.at[0, own, :], loc.at[0]),
        pltpu.make_async_copy(cot, X.at[1, own, :], loc.at[1]),
        pltpu.make_async_copy(upk, wst.at[0], loc.at[2]),
        pltpu.make_async_copy(dnk, wst.at[1], loc.at[3]),
        pltpu.make_async_copy(fst, stg.at[pl.ds(0, 2)], loc.at[4]),
        pltpu.make_async_copy(snd, stg.at[pl.ds(2, 2)], loc.at[5]),
    ]
    for copy in copies:
        copy.start()

    barrier = pltpu.get_barrier_semaphore()

    def greet(sem, dev):
        pl.semaphore_signal(sem, inc=1, device_id=dev, device_id_type=MESH)

    for k in range(1, 8):
        greet(barrier, at(dz=k))
    for k in range(1, 4):
        greet(barrier, at(dx=k))
    greet(barrier, at(dc=1))
    greet(barrier, at(dy=1))
    greet(barrier, at(dy=-1))
    pl.semaphore_wait(barrier, 13)
    for k in range(1, 4):
        greet(row_in, at(dx=k))

    copies[0].wait()
    copies[1].wait()
    for k in range(2):
        send(rows(zl, e, k), rows(zl, e, k), t1s.at[k], t1r.at[k], at(dz=1))
        send(rows(zl, e, 1 - k), rows(zl, e, 1 - k), t1s.at[2 + k], t1r.at[2 + k], at(dz=-1))

    line = lax.broadcasted_iota(jnp.int32, (ROWS, ROWS), 0)
    lane = lax.broadcasted_iota(jnp.int32, (ROWS, ROWS), 1)
    to_block = jnp.zeros((ROWS, ROWS), jnp.int32)
    from_block = jnp.zeros((ROWS, ROWS), jnp.int32)
    for k in range(N):
        here = (lane >> 4) == k
        to_block = jnp.where(here, bd[tg, k], to_block)
        from_block = jnp.where(here, (rank[k] + tg) & 15, from_block)
    within = (line & 15) == (lane & 15)
    order[...] = jnp.where(within & (to_block == (line >> 4)), 1.0, 0.0).astype(BF)
    pick[...] = jnp.where(within & (from_block == (line >> 4)), 1.0, 0.0).astype(BF)

    copies[2].wait()
    copies[3].wait()
    for m in range(2):
        sorted_rows = jnp.dot(order[...], wst[m], preferred_element_type=F32).astype(BF)
        mom[:, 4 + m] = sorted_rows.reshape(N, PIECE, WIDTH)
        wide = jnp.concatenate([sorted_rows, jnp.zeros((ROWS, 128), BF)], axis=1)
        for q in range(4):
            for h in range(2):
                first = q * QUART + h * HALF
                wq[:, q, h, m * PIECE : (m + 1) * PIECE, :] = wide[:, first : first + 128].reshape(
                    N, PIECE, 128
                )

    pl.semaphore_wait(row_in, 3)
    greet(pair_in, at(dc=1))
    pl.semaphore_wait(pair_in, 1)

    me = z * 8 + e

    def send_weights(h):
        def step(k, _):
            to = (me + k) % 64
            nz, nx, nc = to // 8, (to // 2) % 4, to % 2
            nt, nq = (nz // 4) * 8 + nx * 2 + nc, nz % 4
            send(wq.at[nt, nq, h], wr.at[h, zl * N + tg], wqs.at[h], wqr.at[h], (y * 4 + nq, nt))
            return 0

        lax.fori_loop(1, 64, step, 0)
        own_block = pltpu.make_async_copy(wq.at[tg, zl, h], wr.at[h, zl * N + tg], loc.at[10 + h])
        own_block.start()
        return own_block

    own_blocks = [send_weights(0), send_weights(1)]

    came = [(zl + 3) % 4, (zl + 1) % 4, (zl + 2) % 4]

    def spread(p, k):
        half = rows(came[p], e, k)
        send(half, half, t2s.at[p, k], t2r.at[p, k], at(dx=1))
        send(half, half, t2s.at[p, 2 + k], t2r.at[p, 2 + k], at(dx=-1))

    def spread_core(p):
        piece = rows(came[p], e)
        send(piece, piece, t3s.at[p, 0], t3r.at[p, 0], at(dc=1))

    half = rows(came[0], e, 0)
    wait_bytes(half, t1r.at[0])
    send(half, half, t1s.at[4], t1r.at[4], at(dz=1))
    spread(0, 0)
    half = rows(came[1], e, 1)
    wait_bytes(half, t1r.at[2])
    send(half, half, t1s.at[5], t1r.at[5], at(dz=-1))
    spread(1, 1)
    wait_bytes(rows(came[0], e, 1), t1r.at[1])
    spread(0, 1)
    wait_bytes(rows(came[1], e, 0), t1r.at[3])
    spread(1, 0)

    spread_core(0)
    spread_core(1)

    copies[4].wait()
    copies[5].wait()
    for k in range(4):
        sorted_rows = jnp.dot(order[...], stg[k].astype(BF), preferred_element_type=F32)
        mom[:, k] = sorted_rows.astype(BF).reshape(N, PIECE, WIDTH)

    def send_moments(dzh, dx, dc):
        to = (zh + dzh) % 2 * 8 + (x + dx) % 4 * 2 + (c + dc) % 2
        send(mom.at[to], momr.at[tg], ms, mr, (dp, to))

    own_moments = pltpu.make_async_copy(mom.at[tg], momr.at[tg], loc.at[7])
    own_moments.start()


    wait_bytes(rows(came[2], e, 0), t1r.at[4])
    spread(2, 0)
    wait_bytes(rows(came[2], e, 1), t1r.at[5])
    spread(2, 1)
    spread_core(2)

    for h in range(2):
        wait_bytes(wr.at[h, pl.ds(0, 63)], wqr.at[h])
        own_blocks[h].wait()

        def unpack(k, _, h=h):
            for m in range(2):
                block = wr[h, pl.ds(k * N, N), m * PIECE : (m + 1) * PIECE, :].reshape(ROWS, 128)
                turned = lax.dot_general(
                    block, pick[...], (((0,), (1,)), ((), ())), preferred_element_type=F32
                )
                part = pl.ds(pl.multiple_of(k * 256, 256), 256)
                wall[h, y, m, :, part] = turned[:HALF].astype(BF)
            return 0

        lax.fori_loop(0, 4, unpack, 0)
        send(wall.at[h, y], wall.at[h, y], ags.at[h, 0], agr.at[h, 0], at(dy=1))
        send(wall.at[h, y], wall.at[h, y], ags.at[h, 1], agr.at[h, 1], at(dy=-1))

    lax.fori_loop(0, 2, lambda k, _: (send_moments(1, 0, k), 0)[1], 0)

    def near_half(k, _):
        send_moments(1, 1 + k // 2 * 2, k % 2)
        return 0

    left, right, far = (x + 3) % 4 * 2 + c, (x + 1) % 4 * 2 + c, (x + 2) % 4 * 2 + c
    yl, yr, yf = (y + 3) % 4, (y + 1) % 4, (y + 2) % 4

    def pass_x(p):
        half = rows(came[p], left, 0)
        wait_bytes(half, t2r.at[p, 0])
        send(half, half, t2s.at[p, 4], t2r.at[p, 4], at(dx=1))
        half = rows(came[p], right, 1)
        wait_bytes(half, t2r.at[p, 3])
        send(half, half, t2s.at[p, 5], t2r.at[p, 5], at(dx=-1))
        wait_bytes(rows(came[p], left, 1), t2r.at[p, 1])
        piece = rows(came[p], left)
        send(piece, piece, t3s.at[p, 1], t3r.at[p, 1], at(dc=1))
        wait_bytes(rows(came[p], right, 0), t2r.at[p, 2])
        piece = rows(came[p], right)
        send(piece, piece, t3s.at[p, 2], t3r.at[p, 2], at(dc=1))

    def pass_y(h):
        wait_bytes(wall.at[h, yl], agr.at[h, 0])
        send(wall.at[h, yl, 0], wall.at[h, yl, 0], ags.at[h, 2], agr.at[h, 2], at(dy=1))
        wait_bytes(wall.at[h, yr], agr.at[h, 1])
        send(wall.at[h, yr, 1], wall.at[h, yr, 1], ags.at[h, 3], agr.at[h, 3], at(dy=-1))

    def end_x(p):
        wait_bytes(rows(came[p], far, 0), t2r.at[p, 4])
        wait_bytes(rows(came[p], far, 1), t2r.at[p, 5])
        piece = rows(came[p], far)
        send(piece, piece, t3s.at[p, 3], t3r.at[p, 3], at(dc=1))

    def end_tokens(p):
        for k, dx in enumerate((0, 3, 1, 2)):
            wait_bytes(rows(came[p], (x + dx) % 4 * 2 + (1 - c)), t3r.at[p, k])

    def end_y(h):
        wait_bytes(wall.at[h, yf, 0], agr.at[h, 2])
        wait_bytes(wall.at[h, yf, 1], agr.at[h, 3])

    def forward(nz):
        seen = pl.ds(pl.multiple_of(nz * 256, 256), 256)

        def step(ny, _):
            for m in range(2):
                total = jnp.zeros((QUART, 256), F32)
                for k in range(4):
                    cols = pl.ds(pl.multiple_of(ny * CHUNK + k * 256, 256), 256)
                    part = pl.ds(k * 256, 256)
                    weight = jnp.concatenate(
                        [wall[0, ny, m, :, part], wall[1, ny, m, :, part]], axis=0
                    )
                    product = lax.dot_general(
                        weight,
                        X[m, seen, cols],
                        (((1,), (1,)), ((), ())),
                        preferred_element_type=F32,
                    )
                    total += product.astype(BF).astype(F32)
                acc[m] += total
            return 0

        acc[...] = jnp.zeros_like(acc)
        lax.fori_loop(0, 4, step, 0)
        pre, back = acc[0], acc[1]
        sigma = jax.nn.sigmoid(pre)
        act[1, :, seen] = (pre * sigma).astype(BF)
        act[0, :, seen] = (back * sigma * (1.0 + pre * (1.0 - sigma))).astype(BF)

    upper, lower = pl.ds(0, HALF), pl.ds(HALF, HALF)

    def gradient(m, ny):
        def step(i, _):
            cols = pl.ds(pl.multiple_of(ny * CHUNK + i * 256, 256), 256)
            part = pl.ds(pl.multiple_of(i * 256, 256), 256)
            gp[m, ny, :, part] = jnp.dot(
                act[m], X[m, :, cols], preferred_element_type=F32
            ).astype(BF)
            return 0

        lax.fori_loop(0, 4, step, 0)

    def far_gradient(m):
        gradient(m, yf)
        send(gp.at[m, yf, upper], relay.at[m, 0], rss.at[m, 0], rsr.at[m, 0], at(dy=1))
        send(gp.at[m, yf, lower], relay.at[m, 1], rss.at[m, 1], rsr.at[m, 1], at(dy=-1))

    def near_gradients(m):
        gradient(m, yr)
        send(gp.at[m, yr, lower], got.at[m, 0, lower], rss.at[m, 2], rsr.at[m, 2], at(dy=1))
        gradient(m, yl)
        send(gp.at[m, yl, upper], got.at[m, 1, upper], rss.at[m, 3], rsr.at[m, 3], at(dy=-1))

    def relays(m):
        wait_bytes(relay.at[m, 0], rsr.at[m, 0])
        gp[m, yr, upper] = (gp[m, yr, upper].astype(F32) + relay[m, 0].astype(F32)).astype(BF)
        send(gp.at[m, yr, upper], got.at[m, 0, upper], rss.at[m, 4], rsr.at[m, 4], at(dy=1))
        wait_bytes(relay.at[m, 1], rsr.at[m, 1])
        gp[m, yl, lower] = (gp[m, yl, lower].astype(F32) + relay[m, 1].astype(F32)).astype(BF)
        send(gp.at[m, yl, lower], got.at[m, 1, lower], rss.at[m, 5], rsr.at[m, 5], at(dy=-1))

    own_parts = []

    def finish(m):
        wait_bytes(got.at[m, 0, lower], rsr.at[m, 2])
        wait_bytes(got.at[m, 1, upper], rsr.at[m, 3])
        wait_bytes(got.at[m, 0, upper], rsr.at[m, 4])
        wait_bytes(got.at[m, 1, lower], rsr.at[m, 5])
        gsum[m] = (
            gp[m, y].astype(F32) + got[m, 0].astype(F32) + got[m, 1].astype(F32)
        ).astype(BF)
        for k in range(1, 4):
            nq = (zl + k) % 4
            part = gsum.at[m, :, pl.ds(pl.multiple_of(nq * 256, 256), 256)]
            send(part, gout.at[m, zl], zs.at[m, k - 1], zr.at[m, k - 1], (y * 4 + nq, tg))
        own_part = pltpu.make_async_copy(
            gsum.at[m, :, pl.ds(pl.multiple_of(zl * 256, 256), 256)], gout.at[m, zl], loc.at[8 + m]
        )
        own_part.start()
        own_parts.append(own_part)

    pass_x(0)
    pass_x(1)
    pass_y(0)
    pass_x(2)
    lax.fori_loop(0, 4, near_half, 0)
    pass_y(1)
    end_y(0)
    end_y(1)
    forward(zl)
    end_x(0)
    end_x(1)
    end_tokens(0)
    forward(came[0])
    end_x(2)
    lax.fori_loop(0, 2, lambda k, _: (send_moments(1, 2, k), 0)[1], 0)
    for k in range(1, 8):
        send_moments(0, k // 2, k % 2)
    end_tokens(1)
    forward(came[1])
    end_tokens(2)
    forward(came[2])
    far_gradient(0)
    near_gradients(0)
    far_gradient(1)
    relays(0)
    near_gradients(1)
    gradient(0, y)
    gradient(1, y)
    relays(1)
    finish(0)
    finish(1)

    for k in range(6):
        wait_bytes(rows(zl, e, 0), t1s.at[k])
    for p in range(3):
        for k in range(6):
            wait_bytes(rows(zl, e, 0), t2s.at[p, k])
        for k in range(4):
            wait_bytes(rows(zl, e), t3s.at[p, k])
    for h in range(2):
        wait_bytes(wr.at[h, pl.ds(0, 63)], wqs.at[h])
    for h in range(2):
        for k in range(2):
            wait_bytes(wall.at[h, y], ags.at[h, k])
            wait_bytes(wall.at[h, y, 0], ags.at[h, 2 + k])
        for k in range(6):
            wait_bytes(gp.at[h, y, upper], rss.at[h, k])
        for k in range(3):
            wait_bytes(gout.at[h, k], zs.at[h, k])
            wait_bytes(gout.at[h, (zl + 3 - k) % 4], zr.at[h, k])
        own_parts[h].wait()
    wait_bytes(mom.at[pl.ds(0, 15)], ms)
    wait_bytes(momr.at[pl.ds(0, 15)], mr)
    own_moments.wait()


def update(rank, momr, gin, new_up, new_dn, new_first, new_second, grad):
    step = pl.program_id(0)
    tg = lax.axis_index("tensor")

    @pl.when(step == 0)
    def _():
        for m in range(2):
            for q in range(2):
                lanes = pl.ds(q * 128, 128)
                tall = jnp.concatenate([
                    gin[m, k, :, lanes].astype(F32) for k in range(4)
                ], axis=0)
                grad[m, lanes, :] = tall.T

    for half in range(8):
        r = step * 8 + half
        src = jnp.int32(0)
        for k in range(N):
            src = src + jnp.where((rank[k] + tg) % N == r, k, 0)
        at_row = pl.ds(pl.multiple_of(r * PIECE, PIECE), PIECE)
        out_row = pl.ds(half * PIECE, PIECE)
        for m in range(2):
            g = grad[m, at_row, :]
            first = beta_first * momr[src, m].astype(F32) + (1.0 - beta_first) * g
            second = beta_second * momr[src, 2 + m].astype(F32) + (1.0 - beta_second) * g * g
            first_hat = first / (1.0 - beta_first**step_count)
            second_hat = second / (1.0 - beta_second**step_count)
            new = momr[src, 4 + m].astype(F32) - rate * first_hat / (jnp.sqrt(second_hat) + adam_eps)
            new_first[m, out_row, :] = first
            new_second[m, out_row, :] = second
            (new_up, new_dn)[m][out_row, :] = new.astype(BF)


def per_device(tok, cot, upk, dnk, fst, snd, bd, rank):
    anywhere = pl.BlockSpec(memory_space=pl.ANY)
    scalar = pl.BlockSpec(memory_space=pltpu.SMEM)
    dma = pltpu.SemaphoreType.DMA
    momr, gout = pl.pallas_call(
        exchange,
        out_shape=(
            jax.ShapeDtypeStruct((N, 6, PIECE, WIDTH), BF),
            jax.ShapeDtypeStruct((2, 4, QUART, 256), BF),
        ),
        in_specs=[scalar, scalar] + [anywhere] * 6,
        out_specs=(anywhere, anywhere),
        scratch_shapes=[
            pltpu.VMEM((2, TOK, D), BF),
            pltpu.VMEM((4, ROWS, WIDTH), F32),
            pltpu.VMEM((2, ROWS, WIDTH), BF),
            pltpu.VMEM((N, 4, 2, 32, 128), BF),
            pltpu.VMEM((2, 64, 32, 128), BF),
            pltpu.VMEM((N, 6, PIECE, WIDTH), BF),
            pltpu.VMEM((2, 4, 2, HALF, CHUNK), BF),
            pltpu.VMEM((2, QUART, 256), F32),
            pltpu.VMEM((2, QUART, TOK), BF),
            pltpu.VMEM((2, 4, QUART, CHUNK), BF),
            pltpu.VMEM((2, 2, HALF, CHUNK), BF),
            pltpu.VMEM((2, 2, QUART, CHUNK), BF),
            pltpu.VMEM((2, QUART, CHUNK), BF),
            pltpu.VMEM((ROWS, ROWS), BF),
            pltpu.VMEM((ROWS, ROWS), BF),
            pltpu.SemaphoreType.REGULAR,
            pltpu.SemaphoreType.REGULAR,
            dma((12,)),
            dma((6,)),
            dma((6,)),
            dma((3, 6)),
            dma((3, 6)),
            dma((3, 4)),
            dma((3, 4)),
            dma((2,)),
            dma((2,)),
            dma((2, 4)),
            dma((2, 4)),
            dma((2, 6)),
            dma((2, 6)),
            dma,
            dma,
            dma((2, 3)),
            dma((2, 3)),
        ],
        compiler_params=pltpu.CompilerParams(
            has_side_effects=True, collective_id=0, vmem_limit_bytes=60 * 2**20
        ),
        cost_estimate=pl.CostEstimate(
            flops=7_600_000_000, bytes_accessed=20_000_000, transcendentals=500_000
        ),
        name="exchange",
    )(bd, rank, tok, cot, upk, dnk, fst, snd)

    whole = pl.BlockSpec((N, 6, PIECE, WIDTH), lambda i: (0, 0, 0, 0))
    flat = pl.BlockSpec((128, WIDTH), lambda i: (i, 0))
    pair = pl.BlockSpec((2, 128, WIDTH), lambda i: (0, i, 0))
    return pl.pallas_call(
        update,
        grid=(2,),
        out_shape=(
            jax.ShapeDtypeStruct((ROWS, WIDTH), BF),
            jax.ShapeDtypeStruct((ROWS, WIDTH), BF),
            jax.ShapeDtypeStruct((2, ROWS, WIDTH), F32),
            jax.ShapeDtypeStruct((2, ROWS, WIDTH), F32),
        ),
        in_specs=[scalar, whole, pl.BlockSpec((2, 4, QUART, 256), lambda i: (0,) * 4)],
        out_specs=(flat, flat, pair, pair),
        scratch_shapes=[pltpu.VMEM((2, ROWS, WIDTH), F32)],
        compiler_params=pltpu.CompilerParams(vmem_limit_bytes=60 * 2**20),
        cost_estimate=pl.CostEstimate(
            flops=10_000_000, bytes_accessed=13_000_000, transcendentals=500_000
        ),
        name="update",
    )(rank, momr, gout)


def solution(mesh):
    in_specs = (
        P("dp", None),
        P("dp", None),
        P("dp", "tensor"),
        P("dp", "tensor"),
        P(None, "dp", "tensor"),
        P(None, "dp", "tensor"),
        P(),
        P(),
    )
    out_specs = (
        P("dp", "tensor"),
        P("dp", "tensor"),
        P(None, "dp", "tensor"),
        P(None, "dp", "tensor"),
    )
    return jax.shard_map(
        per_device, mesh=mesh, in_specs=in_specs, out_specs=out_specs, check_vma=False
    )
```
